512 devices in a mesh: seq: 512 (over y, z, x, core).
Axes of the slice: x: 4, y: 4, z: 16, core: 2. Of those that a mesh axis runs over, the one named last changes fastest.
Arguments:
- query_rows: bfloat16 [65536, 1024], P('seq'), may hold values from -6 to 6
- key_rows: bfloat16 [65536, 1024], P('seq'), may hold values from -6 to 6
- value_rows: bfloat16 [65536, 1024], P('seq'), may hold values from -6 to 6
- attn_out: bfloat16 [65536, 1024], P('seq'), may hold values from -6 to 6
- out_grad: bfloat16 [65536, 1024], P('seq'), may hold values from -6 to 6
- log_norms: float32 [8, 65536], P(None, 'seq'), may hold values from 2.5 to 4.5
Outputs:
- query_grad: bfloat16 [65536, 1024], P('seq')
- key_grad: bfloat16 [65536, 1024], P('seq')
- value_grad: bfloat16 [65536, 1024], P('seq')
The draws below stay inside these ranges and needn't reach their ends.
All inputs are finite; a program needn't handle non-finite values.
Results may differ from the reference program's by a relative error of at most 0.0049.
Values may be sent and summed in bfloat16 or wider, within the bound.
No kernel may reach another device: no remote copies, remote signals or barrier semaphores. Data moves between devices by JAX's collectives and lax.ppermute only.
A program may use at most 128 MiB of HBM per device.

```python
import jax
import jax.numpy as jnp
from jax import lax

H = 8
HD = 128
TOK_DEV = 128
SPAN_NEAR = 4
SPAN_FAR = 16
SEL = 512
TOKENS = 65536
N_SEQ = 512


def block_levels(rng, extent, shards, least, top_value):
    gain = 1.0
    for position, blocks in shards:
        draws = jax.random.uniform(jax.random.fold_in(jax.random.fold_in(rng, 6), position), (blocks,), jnp.float32, least / len(shards), top_value / len(shards))
        gain = gain * jnp.repeat(jnp.exp(draws), extent[position] // blocks).reshape((-1,) + (1,) * (len(extent) - 1 - position))
    return gain


def bell_draw(key, shape, scale, reach, cuts=(), dtype=jnp.bfloat16):
    gain = block_levels(key, shape, cuts, -0.22, 0.18) if cuts else 1.0
    drawn = jax.random.normal(key, shape, jnp.float32) * scale * gain
    return jnp.minimum(jnp.maximum(drawn, -reach), reach).astype(dtype)


def setup_inputs(seed: int = 0) -> dict:
    key_list = jax.random.split(jax.random.key(seed), 7)
    query_rows = bell_draw(key_list[0], (TOKENS, H * HD), 1.0, 6.0, ((0, 512),))
    key_rows = bell_draw(key_list[1], (TOKENS, H * HD), 1.0, 6.0, ((0, 512),))
    value_rows = bell_draw(key_list[2], (TOKENS, H * HD), 1.0, 6.0, ((0, 512),))
    attn_out = bell_draw(key_list[3], (TOKENS, H * HD), 1.0, 6.0, ((0, 512),))
    out_grad = bell_draw(key_list[4], (TOKENS, H * HD), 1.0, 6.0, ((0, 512),))
    log_norms = jnp.clip(2.5 + 2.0 * jax.random.uniform(key_list[5], (H, TOKENS), jnp.float32) ** block_levels(key_list[5], (H, TOKENS), ((1, 512),), -0.2, 0.2), 2.5, 4.5)
    return dict(query_rows=query_rows, key_rows=key_rows, value_rows=value_rows, attn_out=attn_out, out_grad=out_grad, log_norms=log_norms)


def select_rows(whole, groups, dilation):
    offsets = jnp.arange(H) % dilation
    head_ids = jnp.arange(H)
    shaped = whole.reshape(groups, SEL, dilation, H, HD)
    return shaped[:, :, offsets, head_ids, :]


def select_stats(whole, groups, dilation):
    offsets = jnp.arange(H) % dilation
    head_ids = jnp.arange(H)
    shaped = whole.reshape(H, groups, SEL, dilation)
    picked = shaped[head_ids, :, :, offsets]
    return jnp.transpose(picked, (1, 0, 2))


def group_grads(pieces):
    query, keyset, valueset, gradset, norms, deltas = pieces
    score_scale = HD ** -0.5
    query_f = query.astype(jnp.float32)
    key_f = keyset.astype(jnp.float32)
    value_f = valueset.astype(jnp.float32)
    grad_f = gradset.astype(jnp.float32)
    scores = jnp.einsum('qhd,khd->hqk', query_f, key_f) * score_scale
    causal = jnp.arange(SEL)[:, None] >= jnp.arange(SEL)[None, :]
    probs = jnp.where(causal[None], jnp.exp(scores - norms[:, :, None]), jnp.float32(0.0))
    dprobs = jnp.einsum('qhd,khd->hqk', grad_f, value_f)
    dscores = (probs * (dprobs - deltas[:, :, None])).astype(jnp.bfloat16)
    dscores = lax.optimization_barrier(dscores).astype(jnp.float32)
    probs_low = lax.optimization_barrier(probs.astype(jnp.bfloat16)).astype(jnp.float32)
    grad_query = jnp.einsum('hqk,khd->qhd', dscores, key_f) * score_scale
    grad_key = jnp.einsum('hqk,qhd->khd', dscores, query_f) * score_scale
    grad_value = jnp.einsum('hqk,qhd->khd', probs_low, grad_f)
    return grad_query, grad_key, grad_value


def level_terms(query_rows, key_rows, value_rows, out_grad, log_norms, deltas, span):
    dilation = span // 4
    groups = TOKENS // (span * TOK_DEV)
    pieces = (select_rows(query_rows, groups, dilation), select_rows(key_rows, groups, dilation),
              select_rows(value_rows, groups, dilation), select_rows(out_grad, groups, dilation),
              select_stats(log_norms, groups, dilation), select_stats(deltas, groups, dilation))
    results = lax.map(group_grads, pieces)
    offsets = jnp.arange(H) % dilation
    head_ids = jnp.arange(H)
    placed = []
    for result in results:
        empty = jnp.zeros((groups, SEL, dilation, H, HD), jnp.float32)
        placed.append(empty.at[:, :, offsets, head_ids, :].set(result).reshape(TOKENS, H * HD))
    return placed


def reference(query_rows, key_rows, value_rows, attn_out, out_grad, log_norms):
    product = out_grad.astype(jnp.float32) * attn_out.astype(jnp.float32)
    deltas = jnp.sum(product.reshape(TOKENS, H, HD), axis=-1).T
    totals = [jnp.zeros((TOKENS, H * HD), jnp.float32) for _ in range(3)]
    for span in (SPAN_NEAR, SPAN_FAR, N_SEQ):
        terms = level_terms(query_rows, key_rows, value_rows, out_grad, log_norms, deltas, span)
        totals = [total + term for total, term in zip(totals, terms)]
    return (totals[0].astype(jnp.bfloat16), totals[1].astype(jnp.bfloat16), totals[2].astype(jnp.bfloat16))
```

```python
import functools

import jax
import jax.numpy as jnp
from jax import lax
from jax.experimental import pallas as pl
from jax.experimental.pallas import tpu as pltpu
from jax.sharding import PartitionSpec as P

HEADS = 8
WIDTH = 128
TOK = 128
RING = 8
DEPTH = 16
ROWS = 4
DEVICES = 512
SCALE = WIDTH**-0.5
CHUNK = 4 * TOK + 16
OUT_CHUNK = 3 * TOK
PAIR = 5 * TOK
FAR = 48

BF = jnp.bfloat16
F32 = jnp.float32
VMEM = pl.BlockSpec(memory_space=pltpu.VMEM)
SMEM = pl.BlockSpec(memory_space=pltpu.SMEM)


def iota(shape, dim):
    return lax.broadcasted_iota(jnp.int32, shape, dim)


def dot(a, b):
    return jnp.dot(a, b, preferred_element_type=F32)


def dot_nt(a, b):
    return lax.dot_general(a, b, (((1,), (1,)), ((), ())), preferred_element_type=F32)


def dot_tn(a, b):
    return lax.dot_general(a, b, (((0,), (0,)), ((), ())), preferred_element_type=F32)


def split3(x):
    high = x.astype(BF).astype(F32)
    rest = x - high
    middle = rest.astype(BF).astype(F32)
    low = (rest - middle).astype(BF).astype(F32)
    return high, middle, low


def place3(parts, slot, first):
    high, middle, low = parts
    return jnp.where(
        slot == first,
        high,
        jnp.where(slot == first + 1, middle, jnp.where(slot == first + 2, low, 0.0)),
    )


def position_of(order):
    return 4 * (order % 32) + order // 32


def pre_kernel(q_ref, k_ref, v_ref, o_ref, g_ref, n_ref, near_ref, far_ref):
    perm = (position_of(iota((TOK, TOK), 0)) == iota((TOK, TOK), 1)).astype(BF)
    far_rows = []
    for tensor, ref in enumerate((q_ref, k_ref, v_ref, g_ref)):
        ordered = dot(perm, ref[...]).astype(BF)
        first = ref[0:16, :].astype(F32)
        row = iota((16, WIDTH), 0)
        diagonal = jnp.zeros((16, WIDTH), F32)
        for head in range(HEADS):
            columns = slice(head * WIDTH, (head + 1) * WIDTH)
            near_ref[head, tensor * TOK : (tensor + 1) * TOK, :] = ordered[:, columns]
            diagonal = jnp.where(row == head, first[:, columns], diagonal)
        far_rows.append(diagonal[0:8])
    product = g_ref[...].astype(F32) * o_ref[...].astype(F32)
    lane = iota((TOK, 128), 1)
    spread = jnp.zeros((TOK, 128), F32)
    for head in range(HEADS):
        columns = slice(head * WIDTH, (head + 1) * WIDTH)
        total = jnp.sum(product[:, columns], axis=-1, keepdims=True)
        spread = jnp.where(lane // 16 == head, total, spread)
    deltas = place3(split3(spread), lane % 16, 3)
    norms = jnp.broadcast_to(n_ref[...][:, None, :], (HEADS, 16, TOK)).reshape(128, TOK)
    norms = place3(split3(norms), iota((128, TOK), 0) % 16, 0)
    stat_rows = norms + deltas.T
    stat_columns = deltas + norms.T
    ordered_stats = dot_nt(stat_rows.astype(BF), perm).astype(BF)
    for head in range(HEADS):
        near_ref[head, 4 * TOK : CHUNK, :] = ordered_stats[head * 16 : (head + 1) * 16, :]
    far_stats = jnp.sum(
        jnp.where(iota((TOK, 128), 0) == lane // 16, stat_columns, 0.0), axis=0, keepdims=True
    )
    far_rows.append(jnp.where(iota((16, 128), 0) == 0, far_stats, 0.0))
    payload = jnp.concatenate(far_rows, axis=0).astype(BF)
    for layer in range(DEPTH):
        far_ref[layer] = payload


def far_kernel(i_ref, r_ref, s_ref, flat):
    index = i_ref[0]
    row = index // 128
    layer = (index // 8) % DEPTH
    place = index % RING
    flat[...] = r_ref[...].astype(F32).reshape(DEPTH * FAR, WIDTH)
    stats = flat[pl.ds(32, DEPTH, stride=FAR), :].astype(BF)
    spot = (iota((DEPTH, 128), 1) == place * 16 + iota((DEPTH, 128), 0)).astype(BF)
    stat_tiles = dot_tn(stats, spot)
    depth = iota((DEPTH, WIDTH), 0)
    tile_row = iota((16, WIDTH), 0)
    for head in range(HEADS):
        query, key, value, grad = [
            flat[pl.ds(tensor * 8 + head, DEPTH, stride=FAR), :] for tensor in range(4)
        ]
        extra = stat_tiles[head * 16 : (head + 1) * 16, :]
        for tensor in range(4):
            own = flat[pl.ds(layer * FAR + tensor * 8 + head, 1), :]
            extra = jnp.where(tile_row == 8 + tensor, own, extra)
        extra = extra.astype(BF)
        for target in range(ROWS):
            cut = jnp.where(row < target, DEPTH, jnp.where(row == target, layer, 0))
            earlier = depth < cut
            chunk = target * RING + head
            s_ref[chunk, 0:16, :] = jnp.where(earlier, key, query).astype(BF)
            s_ref[chunk, 16:32, :] = jnp.where(earlier, value, grad).astype(BF)
            s_ref[chunk, 32:48, :] = extra


def pair_kernel(i_ref, r_ref, p_ref):
    index = i_ref[0]
    upper = (index // 8) % 2 == 1
    offset = 32 * (index % 4)
    first = jnp.where(upper, 0, TOK)
    second = jnp.where(upper, 3 * TOK, 2 * TOK)
    for number, start in enumerate((first, second)):
        start = pl.multiple_of(start + offset, 32)
        p_ref[number * 256 : (number + 1) * 256, :] = r_ref[:, pl.ds(start, 32), :].reshape(
            256, WIDTH
        )
    p_ref[512:640, :] = r_ref[:, 4 * TOK : CHUNK, :].reshape(128, 128)


def stat_pair(tile):
    norm = tile[0:1] + tile[1:2] + tile[2:3]
    delta = tile[3:4] + tile[4:5] + tile[5:6]
    return norm, delta


def block_terms(query, key, value, grad, norm, delta, mask):
    scores = dot_nt(key, query) * SCALE
    probs = jnp.exp(scores - norm)
    if mask is not None:
        probs = jnp.where(mask, probs, 0.0)
    dprobs = dot_nt(value, grad)
    dscores = (probs * (dprobs - delta)).astype(BF)
    return probs.astype(BF), dscores


def near_kernel(r_ref, o_ref):
    half = 256
    for segment in range(2):
        base = segment * 4

        def rows(tensor, first, count):
            part = r_ref[base + first : base + first + count, tensor * TOK : (tensor + 1) * TOK, :]
            return part.reshape(count * TOK, WIDTH)

        tiles = [r_ref[base + s, 4 * TOK : CHUNK, :].astype(F32) for s in range(4)]
        key_sum = [None, None]
        value_sum = [None, None]
        for block in range(2):
            count = (block + 1) * 2
            size = count * TOK
            query = rows(0, block * 2, 2)
            grad = rows(3, block * 2, 2)
            key = rows(1, 0, count)
            value = rows(2, 0, count)
            stats = [stat_pair(tiles[block * 2 + s]) for s in range(2)]
            norm = jnp.concatenate([s[0] for s in stats], axis=1)
            delta = jnp.concatenate([s[1] for s in stats], axis=1)
            key_order = iota((size, half), 0)
            query_order = iota((size, half), 1)
            key_place = key_order // TOK * TOK + position_of(key_order % TOK)
            query_place = (
                block * half + query_order // TOK * TOK + position_of(query_order % TOK)
            )
            probs, dscores = block_terms(
                query, key, value, grad, norm, delta, key_place <= query_place
            )
            query_grad = dot_tn(dscores, key) * SCALE
            o_ref[base + block * 2 : base + block * 2 + 2, 0:TOK, :] = query_grad.reshape(
                2, TOK, WIDTH
            )
            key_part = dot(dscores, query) * SCALE
            value_part = dot(probs, grad)
            for number in range(block + 1):
                piece = slice(number * half, (number + 1) * half)
                first = number == block
                key_sum[number] = key_part[piece] if first else key_sum[number] + key_part[piece]
                value_sum[number] = (
                    value_part[piece] if first else value_sum[number] + value_part[piece]
                )
        for number in range(2):
            span = slice(base + number * 2, base + number * 2 + 2)
            o_ref[span, TOK : 2 * TOK, :] = key_sum[number].reshape(2, TOK, WIDTH)
            o_ref[span, 2 * TOK : 3 * TOK, :] = value_sum[number].reshape(2, TOK, WIDTH)


def join_kernel(i_ref, r_ref, x_ref, f_ref, n_ref, o_ref, sums, wide):
    index = i_ref[0]
    row = index // 128
    layer = (index // 8) % DEPTH
    place = index % RING
    upper = layer % 2 == 1
    offset = pl.multiple_of(32 * (index % 4), 32)
    sums[...] = n_ref[...]

    def add(tensor, part):
        span = pl.ds(pl.multiple_of(tensor * TOK + offset, 32), 32)
        sums[:, span, :] = sums[:, span, :] + part.reshape(RING, 32, WIDTH)

    def own(tensor):
        start = pl.multiple_of(tensor * TOK + offset, 32)
        return r_ref[:, pl.ds(start, 32), :].reshape(256, WIDTH)

    lane_from = iota((1024, 256), 0)
    lane_to = iota((1024, 256), 1)
    spot = (lane_from == lane_to // 32 * TOK + offset + lane_to % 32).astype(BF)
    own_tiles = jnp.concatenate([r_ref[s, 4 * TOK : CHUNK, :] for s in range(RING)], axis=1)
    own_norm, own_delta = stat_pair(dot(own_tiles, spot))
    query, key, value, grad = own(0), own(1), own(2), own(3)
    causal = iota((256, 256), 0) <= iota((256, 256), 1)
    probs, dscores = block_terms(query, key, value, grad, own_norm, own_delta, causal)
    add(0, dot_tn(dscores, key) * SCALE)
    add(1, dot(dscores, query) * SCALE)
    add(2, dot(probs, grad))

    @pl.when(upper)
    def _():
        far_key = x_ref[0:256, :]
        far_value = x_ref[256:512, :]
        _, dscores = block_terms(query, far_key, far_value, grad, own_norm, own_delta, None)
        add(0, dot_tn(dscores, far_key) * SCALE)

    @pl.when(jnp.logical_not(upper))
    def _():
        far_query = x_ref[0:256, :]
        far_grad = x_ref[256:512, :]
        far_tiles = jnp.concatenate(
            [x_ref[512 + s * 16 : 528 + s * 16, :] for s in range(RING)], axis=1
        )
        far_norm, far_delta = stat_pair(dot(far_tiles, spot))
        probs, dscores = block_terms(far_query, key, value, far_grad, far_norm, far_delta, None)
        add(1, dot(dscores, far_query) * SCALE)
        add(2, dot(probs, far_grad))

    extras = f_ref[:, 32:48, :].astype(F32)
    stat_rows = []
    for y in range(ROWS):
        stat_rows.append(jnp.sum(extras[y * RING : (y + 1) * RING], axis=0))
    norm_row, delta_row = stat_pair(jnp.concatenate(stat_rows, axis=1))
    wide[...] = f_ref[pl.ds(row * RING, RING), 32:48, :].astype(F32).reshape(128, 128)
    mine = [wide[pl.ds(8 + tensor, RING, stride=16), :] for tensor in range(4)]
    lane8 = iota((8, 512), 1)
    seat8 = iota((8, 512), 0)
    chosen = lane8 == row * 128 + seat8 * 16 + layer
    norm_column = jnp.sum(jnp.where(chosen, norm_row, 0.0), axis=1, keepdims=True)
    delta_column = jnp.sum(jnp.where(chosen, delta_row, 0.0), axis=1, keepdims=True)
    tail_lane = iota((8, 128), 1)
    tail_seat = iota((8, 128), 0)
    on_tail = tail_lane == 8 + tail_seat
    norm_tail = jnp.sum(jnp.where(on_tail, norm_column, 0.0), axis=0, keepdims=True)
    delta_tail = jnp.sum(jnp.where(on_tail, delta_column, 0.0), axis=0, keepdims=True)
    pad = jnp.zeros((112, WIDTH), F32)
    near_a = jnp.concatenate([mine[1], mine[0], pad], axis=0).astype(BF)
    near_b = jnp.concatenate([mine[2], mine[3], pad], axis=0).astype(BF)
    all_a = jnp.concatenate([f_ref[:, 0:16, :].reshape(512, WIDTH), near_a], axis=0)
    all_b = jnp.concatenate([f_ref[:, 16:32, :].reshape(512, WIDTH), near_b], axis=0)
    left = jnp.concatenate([mine[0], mine[1]], axis=0).astype(BF)
    right = jnp.concatenate([mine[3], mine[2]], axis=0).astype(BF)
    scores = dot_nt(left, all_a) * SCALE
    dprobs = dot_nt(right, all_b)
    norm_wide = jnp.concatenate([norm_row, norm_tail], axis=1)
    delta_wide = jnp.concatenate([delta_row, delta_tail], axis=1)
    norms = jnp.concatenate(
        [jnp.broadcast_to(norm_column, (8, 640)), jnp.broadcast_to(norm_wide, (8, 640))], axis=0
    )
    deltas = jnp.concatenate(
        [jnp.broadcast_to(delta_column, (8, 640)), jnp.broadcast_to(delta_wide, (8, 640))], axis=0
    )
    lane = iota((16, 640), 1)
    seat = iota((16, 640), 0)
    source = lane // 128 * DEPTH + lane % DEPTH
    here = row * DEPTH + layer
    tail = lane - 512
    low = jnp.where(lane < 512, source, jnp.where(tail < 8, here - 1 + (tail > seat), 1 << 20))
    high = jnp.where(lane < 512, source, jnp.where((tail >= 8) & (tail < 16), here + 1 - (tail < seat), -1))
    valid = ((seat < 8) & (low < here)) | ((seat >= 8) & (high > here))
    probs = jnp.where(valid, jnp.exp(jnp.where(valid, scores - norms, 0.0)), 0.0)
    dscores = (probs * (dprobs - deltas)).astype(BF)
    by_a = dot(dscores, all_a) * SCALE
    by_b = dot(probs.astype(BF), all_b)
    wide[0:16, :] = by_a
    wide[16:32, :] = by_b
    spot_row = offset + place // 4
    for s in range(RING):
        for tensor, at in ((0, s), (1, 8 + s), (2, 24 + s)):
            span = pl.ds(tensor * TOK + spot_row, 1)
            sums[s, span, :] = sums[s, span, :] + wide[at : at + 1, :]
    o_ref[...] = sums[...].astype(BF)


def post_kernel(r_ref, q_ref, k_ref, v_ref):
    back = (position_of(iota((TOK, TOK), 1)) == iota((TOK, TOK), 0)).astype(BF)
    for tensor, ref in enumerate((q_ref, k_ref, v_ref)):
        for head in range(HEADS):
            part = r_ref[head, tensor * TOK : (tensor + 1) * TOK, :]
            ref[:, head * WIDTH : (head + 1) * WIDTH] = dot(back, part).astype(BF)


def call(kernel, name, out, specs, scratch=(), flops=0, moved=0):
    return pl.pallas_call(
        kernel,
        name=name,
        out_shape=out,
        in_specs=specs,
        out_specs=jax.tree.map(lambda _: VMEM, out),
        scratch_shapes=list(scratch),
        cost_estimate=pl.CostEstimate(flops=flops, bytes_accessed=moved, transcendentals=0),
        compiler_params=pltpu.CompilerParams(vmem_limit_bytes=40 * 1024 * 1024),
    )


def shape(dims, dtype=BF):
    return jax.ShapeDtypeStruct(dims, dtype)


RING_GROUPS = [[base + i for i in range(RING)] for base in range(0, DEVICES, RING)]
DEPTH_GROUPS = [
    [y * 128 + z * 8 + i for z in range(DEPTH)] for y in range(ROWS) for i in range(RING)
]
FLAT_GROUPS = [
    [y * 128 + z * 8 + i for y in range(ROWS) for i in range(RING)] for z in range(DEPTH)
]


def exchange(array, groups):
    return lax.all_to_all(array, "seq", 0, 0, axis_index_groups=groups, tiled=True)


def body(query_rows, key_rows, value_rows, attn_out, out_grad, log_norms):
    index = lax.axis_index("seq").astype(jnp.int32).reshape(1)
    near, far = call(
        pre_kernel,
        "reorder",
        (shape((HEADS, CHUNK, WIDTH)), shape((DEPTH, FAR, WIDTH))),
        [VMEM] * 6,
        flops=2 * 128 * 128 * 4096,
        moved=3 << 20,
    )(query_rows, key_rows, value_rows, attn_out, out_grad, log_norms)
    far = exchange(far, DEPTH_GROUPS)
    near = exchange(near, RING_GROUPS)
    far = call(
        far_kernel,
        "far_middle",
        shape((ROWS * RING, FAR, WIDTH)),
        [SMEM, VMEM],
        [pltpu.VMEM((DEPTH * FAR, WIDTH), F32)],
        moved=1 << 20,
    )(index, far)
    far = exchange(far, FLAT_GROUPS)
    pair = call(pair_kernel, "pair_rows", shape((PAIR, WIDTH)), [SMEM, VMEM], moved=1 << 18)(
        index, near
    )
    pair = lax.ppermute(pair, "seq", [(i, i ^ 8) for i in range(DEVICES)])
    sums = call(
        near_kernel,
        "near_grads",
        shape((RING, OUT_CHUNK, WIDTH), F32),
        [VMEM],
        flops=2 * 10 * 128 * 512 * 384,
        moved=3 << 20,
    )(near)
    grads = call(
        join_kernel,
        "join_grads",
        shape((RING, OUT_CHUNK, WIDTH)),
        [SMEM, VMEM, VMEM, VMEM, VMEM],
        [pltpu.VMEM((RING, OUT_CHUNK, WIDTH), F32), pltpu.VMEM((128, 128), F32)],
        flops=2 * 10 * 128 * 256 * 256,
        moved=4 << 20,
    )(index, near, pair, far, sums)
    grads = exchange(grads, RING_GROUPS)
    out = shape((TOK, HEADS * WIDTH))
    return call(
        post_kernel, "restore", (out, out, out), [VMEM], flops=2 * 128 * 128 * 3072, moved=2 << 20
    )(grads)


def solution(mesh):
    return jax.shard_map(
        body,
        mesh=mesh,
        in_specs=(
            P("seq", None),
            P("seq", None),
            P("seq", None),
            P("seq", None),
            P("seq", None),
            P(None, "seq"),
        ),
        out_specs=(P("seq", None), P("seq", None), P("seq", None)),
        check_vma=False,
    )
```

```python
import functools

import jax
import jax.numpy as jnp
from jax import lax
from jax.experimental import pallas as pl
from jax.experimental.pallas import tpu as pltpu
from jax.sharding import PartitionSpec as P

HEADS = 8
WIDTH = 128
TOK = 128
RING = 8
DEPTH = 16
ROWS = 4
DEVICES = 512
SCALE = WIDTH**-0.5
SIDE = 32
CHUNK = 4 * SIDE + 16
OUT_CHUNK = 3 * SIDE
PAIR = 4 * 128 + 32
FAR = 48
PLANE = 2 * 128 + 16
NEAR = 2 * TOK + 16

BF = jnp.bfloat16
F32 = jnp.float32
VMEM = pl.BlockSpec(memory_space=pltpu.VMEM)
SMEM = pl.BlockSpec(memory_space=pltpu.SMEM)
ANY = pl.BlockSpec(memory_space=pl.ANY)


def iota(shape, dim):
    return lax.broadcasted_iota(jnp.int32, shape, dim)


def dot(a, b):
    return jnp.dot(a, b, preferred_element_type=F32)


def dot_nt(a, b):
    return lax.dot_general(a, b, (((1,), (1,)), ((), ())), preferred_element_type=F32)


def dot_tn(a, b):
    return lax.dot_general(a, b, (((0,), (0,)), ((), ())), preferred_element_type=F32)


def split3(x):
    high = x.astype(BF).astype(F32)
    rest = x - high
    middle = rest.astype(BF).astype(F32)
    low = (rest - middle).astype(BF).astype(F32)
    return high, middle, low


def place3(parts, slot, first):
    high, middle, low = parts
    return jnp.where(
        slot == first,
        high,
        jnp.where(slot == first + 1, middle, jnp.where(slot == first + 2, low, 0.0)),
    )


def columns_of(head):
    return slice(head * WIDTH, (head + 1) * WIDTH)


def stat_pair(tile):
    norm = tile[0:1] + tile[1:2] + tile[2:3]
    delta = tile[3:4] + tile[4:5] + tile[5:6]
    return norm, delta


def block_terms(query, key, value, grad, norm, delta, mask):
    scores = dot_nt(key, query) * SCALE
    probs = jnp.exp(scores - norm)
    if mask is not None:
        probs = jnp.where(mask, probs, 0.0)
    dprobs = dot_nt(value, grad)
    dscores = (probs * (dprobs - delta)).astype(BF)
    return probs.astype(BF), dscores


def select_kernel(i_ref, q_in, k_in, v_in, g_in, o_in, n_in, out_ref, stat_ref, q, k, v, g, o, n, sems):
    sources = (n_in, g_in, o_in, q_in, k_in, v_in)
    places = (n, g, o, q, k, v)
    copies = [
        pltpu.make_async_copy(source, place, sems.at[number])
        for number, (source, place) in enumerate(zip(sources, places))
    ]
    for copy in copies:
        copy.start()
    seat = i_ref[0] % RING
    copies[0].wait()
    copies[1].wait()
    copies[2].wait()
    lane = iota((TOK, 128), 1)
    spread = jnp.zeros((TOK, 128), F32)
    for head in range(HEADS):
        product = g[:, columns_of(head)].astype(F32) * o[:, columns_of(head)].astype(F32)
        total = jnp.sum(product, axis=-1, keepdims=True)
        spread = jnp.where(lane // 16 == head, total, spread)
    deltas = place3(split3(spread), lane % 16, 3)
    norms = jnp.broadcast_to(n[...][:, None, :], (HEADS, 16, TOK)).reshape(128, TOK)
    norms = place3(split3(norms), iota((128, TOK), 0) % 16, 0)
    stats = (norms + deltas.T).astype(BF)
    for head in range(HEADS):
        stat_ref[:, columns_of(head)] = stats[head * 16 : (head + 1) * 16, :]
    token = iota((TOK, 128), 0)
    for residue in range(4):
        spot = ((token == 4 * (lane % SIDE) + residue) & (lane // SIDE == seat % 4)).astype(BF)
        placed = dot(stats, spot).astype(BF)
        for head in (residue, residue + 4):
            out_ref[head, 4 * SIDE : CHUNK, :] = placed[head * 16 : (head + 1) * 16, :]
    order = iota((TOK, TOK), 0)
    perm = (4 * (order % SIDE) + order // SIDE == iota((TOK, TOK), 1)).astype(BF)
    for tensor, (ref, copy) in enumerate(
        ((q, copies[3]), (k, copies[4]), (v, copies[5]), (g, None))
    ):
        if copy is not None:
            copy.wait()
        ordered = dot(perm, ref[...]).astype(BF)
        for head in range(HEADS):
            start = SIDE * (head % 4)
            out_ref[head, tensor * SIDE : (tensor + 1) * SIDE, :] = ordered[
                start : start + SIDE, columns_of(head)
            ]


def payload_kernel(i_ref, q_in, k_in, v_in, g_in, s_in, core_ref, chip_ref, sems):
    index = i_ref[0]
    for number, (ref, bit) in enumerate(((core_ref, 1), (chip_ref, 2))):
        later = (index & bit) != 0

        def send(first, second, ref=ref, number=number):
            copies = [
                pltpu.make_async_copy(first, ref.at[pl.ds(0, TOK)], sems.at[number, 0]),
                pltpu.make_async_copy(second, ref.at[pl.ds(TOK, TOK)], sems.at[number, 1]),
                pltpu.make_async_copy(s_in, ref.at[pl.ds(2 * TOK, 16)], sems.at[number, 2]),
            ]
            for copy in copies:
                copy.start()
            for copy in copies:
                copy.wait()

        @pl.when(later)
        def _():
            send(q_in, g_in)

        @pl.when(jnp.logical_not(later))
        def _():
            send(k_in, v_in)


def near_kernel(i_ref, q, k, v, g, s, r1, r2, r3, after, dq, dk, dv):
    index = i_ref[0]
    core = (index & 1) == 1
    chip = (index & 2) == 2
    causal = iota((TOK, TOK), 0) <= iota((TOK, TOK), 1)
    own_stats = [stat_pair(s[:, columns_of(head)].astype(F32)) for head in range(HEADS)]
    for head in range(HEADS):
        c = columns_of(head)
        norm, delta = own_stats[head]
        probs, dscores = block_terms(q[:, c], k[:, c], v[:, c], g[:, c], norm, delta, causal)
        dq[:, c] = dot_tn(dscores, k[:, c]) * SCALE
        dk[:, c] = dot(dscores, q[:, c]) * SCALE
        dv[:, c] = dot(probs, g[:, c])

    def from_keys(refs):
        for head in range(HEADS):
            c = columns_of(head)
            norm, delta = own_stats[head]
            key = jnp.concatenate([ref[0:TOK, c] for ref in refs], axis=0)
            value = jnp.concatenate([ref[TOK : 2 * TOK, c] for ref in refs], axis=0)
            _, dscores = block_terms(q[:, c], key, value, g[:, c], norm, delta, None)
            dq[:, c] = dq[:, c] + dot_tn(dscores, key) * SCALE

    def from_queries(refs):
        for head in range(HEADS):
            c = columns_of(head)
            query = jnp.concatenate([ref[0:TOK, c] for ref in refs], axis=0)
            grad = jnp.concatenate([ref[TOK : 2 * TOK, c] for ref in refs], axis=0)
            tile = jnp.concatenate([ref[2 * TOK : NEAR, c] for ref in refs], axis=1).astype(F32)
            norm, delta = stat_pair(tile)
            probs, dscores = block_terms(query, k[:, c], v[:, c], grad, norm, delta, None)
            dk[:, c] = dk[:, c] + dot(dscores, query) * SCALE
            dv[:, c] = dv[:, c] + dot(probs, grad)

    for later, refs in ((core, (r1,)), (chip, (r2, r3))):

        @pl.when(later)
        def _(refs=refs):
            from_keys(refs)

        @pl.when(jnp.logical_not(later))
        def _(refs=refs):
            from_queries(refs)


def middle_kernel(i_ref, r_ref, far_ref, pair_ref, flat):
    index = i_ref[0]
    layer = (index // 8) % DEPTH
    place = index % RING
    upper = layer % 2 == 1
    lane = iota((16, 128), 1)
    tiles = [r_ref[s, 4 * SIDE : CHUNK, :].astype(F32) for s in range(RING)]
    stats = jnp.zeros((16, 128), F32)
    for s in range(RING):
        taken = jnp.where(lane == (s % 4) * SIDE + place // 4, tiles[s], 0.0)
        value = jnp.sum(taken, axis=1, keepdims=True)
        stats = jnp.where(lane == layer * RING + s, value, stats)
    rows = []
    for tensor in range(4):
        flat[...] = r_ref[:, tensor * SIDE : tensor * SIDE + 16, :].astype(F32).reshape(128, WIDTH)
        rows.append(flat[pl.ds(place // 4, RING, stride=16), :])
    payload = jnp.concatenate(rows + [stats], axis=0).astype(BF)
    for target in range(DEPTH):
        far_ref[target] = payload

    def fill(first, second):
        for number, tensor in enumerate((first, second)):
            pair_ref[number * 256 : (number + 1) * 256, :] = r_ref[
                :, tensor * SIDE : (tensor + 1) * SIDE, :
            ].reshape(256, WIDTH)

    @pl.when(upper)
    def _():
        fill(0, 3)

    @pl.when(jnp.logical_not(upper))
    def _():
        fill(1, 2)

    pair_ref[512:528, :] = (tiles[0] + tiles[1] + tiles[2] + tiles[3]).astype(BF)
    pair_ref[528:544, :] = (tiles[4] + tiles[5] + tiles[6] + tiles[7]).astype(BF)


def pair_kernel(i_ref, r_ref, x_ref, o_ref):
    upper = (i_ref[0] // 8) % 2 == 1

    def own(tensor):
        return r_ref[:, tensor * SIDE : (tensor + 1) * SIDE, :].reshape(256, WIDTH)

    def put(tensor, part):
        o_ref[:, tensor * SIDE : (tensor + 1) * SIDE, :] = part.reshape(RING, SIDE, WIDTH)

    def add(tensor, part):
        span = slice(tensor * SIDE, (tensor + 1) * SIDE)
        o_ref[:, span, :] = o_ref[:, span, :] + part.reshape(RING, SIDE, WIDTH)

    tiles = [r_ref[s, 4 * SIDE : CHUNK, :].astype(F32) for s in range(RING)]
    own_tile = jnp.concatenate(
        [tiles[0] + tiles[1] + tiles[2] + tiles[3], tiles[4] + tiles[5] + tiles[6] + tiles[7]],
        axis=1,
    )
    norm, delta = stat_pair(own_tile)
    query, key, value, grad = own(0), own(1), own(2), own(3)
    causal = iota((256, 256), 0) <= iota((256, 256), 1)
    probs, dscores = block_terms(query, key, value, grad, norm, delta, causal)
    put(0, dot_tn(dscores, key) * SCALE)
    put(1, dot(dscores, query) * SCALE)
    put(2, dot(probs, grad))

    @pl.when(upper)
    def _():
        far_key = x_ref[0:256, :]
        far_value = x_ref[256:512, :]
        _, dscores = block_terms(query, far_key, far_value, grad, norm, delta, None)
        add(0, dot_tn(dscores, far_key) * SCALE)

    @pl.when(jnp.logical_not(upper))
    def _():
        far_query = x_ref[0:256, :]
        far_grad = x_ref[256:512, :]
        far_tile = jnp.concatenate([x_ref[512:528, :], x_ref[528:544, :]], axis=1).astype(F32)
        far_norm, far_delta = stat_pair(far_tile)
        probs, dscores = block_terms(far_query, key, value, far_grad, far_norm, far_delta, None)
        add(1, dot(dscores, far_query) * SCALE)
        add(2, dot(probs, far_grad))


def plane_kernel(i_ref, r_ref, after_pair, o_ref):
    index = i_ref[0]
    row = index // 128
    layer = (index // 8) % DEPTH
    held = r_ref[...].astype(F32)
    query, key, value, grad = [
        held[:, tensor * 8 : (tensor + 1) * 8, :].reshape(128, WIDTH) for tensor in range(4)
    ]
    tile = jnp.sum(held[:, 32:48, :], axis=0).astype(BF)
    depth = iota((128, WIDTH), 0) // RING
    for target in range(ROWS):
        cut = jnp.where(row < target, DEPTH, jnp.where(row == target, layer, 0))
        earlier = depth < cut
        o_ref[target, 0:128, :] = jnp.where(earlier, key, query).astype(BF)
        o_ref[target, 128:256, :] = jnp.where(earlier, value, grad).astype(BF)
        o_ref[target, 256:PLANE, :] = tile


def join_kernel(i_ref, f_ref, m_ref, n_ref, after, o_ref, sums, wide):
    index = i_ref[0]
    row = index // 128
    layer = (index // 8) % DEPTH
    place = index % RING
    here = row * DEPTH + layer
    sums[...] = n_ref[...]
    mine_all = m_ref[0].astype(F32)
    mine = [mine_all[tensor * 8 : (tensor + 1) * 8] for tensor in range(4)]
    stat_rows = [f_ref[y, 256:PLANE, :].astype(F32) for y in range(ROWS)]
    norm_row, delta_row = stat_pair(jnp.concatenate(stat_rows, axis=1))
    chosen = iota((8, 512), 1) == here * RING + iota((8, 512), 0)
    norm_column = jnp.sum(jnp.where(chosen, norm_row, 0.0), axis=1, keepdims=True)
    delta_column = jnp.sum(jnp.where(chosen, delta_row, 0.0), axis=1, keepdims=True)
    on_tail = iota((8, 128), 1) == 8 + iota((8, 128), 0)
    norm_tail = jnp.sum(jnp.where(on_tail, norm_column, 0.0), axis=0, keepdims=True)
    delta_tail = jnp.sum(jnp.where(on_tail, delta_column, 0.0), axis=0, keepdims=True)
    pad = jnp.zeros((112, WIDTH), F32)
    near_a = jnp.concatenate([mine[1], mine[0], pad], axis=0).astype(BF)
    near_b = jnp.concatenate([mine[2], mine[3], pad], axis=0).astype(BF)
    all_a = jnp.concatenate([f_ref[y, 0:128, :] for y in range(ROWS)] + [near_a], axis=0)
    all_b = jnp.concatenate([f_ref[y, 128:256, :] for y in range(ROWS)] + [near_b], axis=0)
    left = jnp.concatenate([mine[0], mine[1]], axis=0).astype(BF)
    right = jnp.concatenate([mine[3], mine[2]], axis=0).astype(BF)
    scores = dot_nt(left, all_a) * SCALE
    dprobs = dot_nt(right, all_b)
    norm_wide = jnp.concatenate([norm_row, norm_tail], axis=1)
    delta_wide = jnp.concatenate([delta_row, delta_tail], axis=1)
    norms = jnp.concatenate(
        [jnp.broadcast_to(norm_column, (8, 640)), jnp.broadcast_to(norm_wide, (8, 640))], axis=0
    )
    deltas = jnp.concatenate(
        [jnp.broadcast_to(delta_column, (8, 640)), jnp.broadcast_to(delta_wide, (8, 640))], axis=0
    )
    lane = iota((16, 640), 1)
    seat = iota((16, 640), 0)
    source = lane // RING
    tail = lane - 512
    low = jnp.where(lane < 512, source, jnp.where(tail < 8, here - 1 + (tail > seat), 1 << 20))
    high = jnp.where(
        lane < 512, source, jnp.where((tail >= 8) & (tail < 16), here + 1 - (tail < seat), -1)
    )
    valid = ((seat < 8) & (low < here)) | ((seat >= 8) & (high > here))
    probs = jnp.where(valid, jnp.exp(jnp.where(valid, scores - norms, 0.0)), 0.0)
    dscores = (probs * (dprobs - deltas)).astype(BF)
    wide[0:16, :] = dot(dscores, all_a) * SCALE
    wide[16:32, :] = dot(probs.astype(BF), all_b)
    for s in range(RING):
        for tensor, at in ((0, s), (1, 8 + s), (2, 24 + s)):
            span = pl.ds(tensor * SIDE + place // 4, 1)
            sums[s, span, :] = sums[s, span, :] + wide[at : at + 1, :]
    o_ref[...] = sums[...].astype(BF)


def post_kernel(r_ref, dq, dk, dv, q_ref, k_ref, v_ref):
    for tensor, (near, ref) in enumerate(((dq, q_ref), (dk, k_ref), (dv, v_ref))):
        for head in range(HEADS):
            residue = head % 4
            back = (iota((TOK, SIDE), 0) == 4 * iota((TOK, SIDE), 1) + residue).astype(BF)
            part = dot(back, r_ref[head, tensor * SIDE : (tensor + 1) * SIDE, :])
            ref[:, columns_of(head)] = (near[:, columns_of(head)] + part).astype(BF)


def call(kernel, name, out, specs, scratch=(), flops=0, moved=0, places=None, limit=16):
    return pl.pallas_call(
        kernel,
        name=name,
        out_shape=out,
        in_specs=specs,
        out_specs=jax.tree.map(lambda _: VMEM, out) if places is None else places,
        scratch_shapes=list(scratch),
        cost_estimate=pl.CostEstimate(flops=flops, bytes_accessed=moved, transcendentals=0),
        compiler_params=pltpu.CompilerParams(vmem_limit_bytes=limit * 1024 * 1024),
    )


def shape(dims, dtype=BF):
    return jax.ShapeDtypeStruct(dims, dtype)


RING_GROUPS = [[base + i for i in range(RING)] for base in range(0, DEVICES, RING)]
DEPTH_GROUPS = [
    [y * 128 + z * 8 + i for z in range(DEPTH)] for y in range(ROWS) for i in range(RING)
]
ROW_GROUPS = [[y * 128 + i for y in range(ROWS)] for i in range(128)]


def exchange(array, groups):
    return lax.all_to_all(array, "seq", 0, 0, axis_index_groups=groups, tiled=True)


def partner(array, bit):
    return lax.ppermute(array, "seq", [(i, i ^ bit) for i in range(DEVICES)])


def body(query_rows, key_rows, value_rows, attn_out, out_grad, log_norms):
    index = lax.axis_index("seq").astype(jnp.int32).reshape(1)
    whole = (TOK, HEADS * WIDTH)
    side, stats = call(
        select_kernel,
        "select_rows",
        (shape((HEADS, CHUNK, WIDTH)), shape((16, HEADS * WIDTH))),
        [SMEM] + [ANY] * 6,
        [pltpu.VMEM(whole, BF)] * 5
        + [pltpu.VMEM((HEADS, TOK), F32), pltpu.SemaphoreType.DMA((6,))],
        flops=2 * 128 * 128 * 4096,
        moved=3 << 20,
        limit=60,
    )(index, query_rows, key_rows, value_rows, out_grad, attn_out, log_norms)
    side = exchange(side, RING_GROUPS)
    core, chip = call(
        payload_kernel,
        "near_payload",
        (shape((NEAR, HEADS * WIDTH)), shape((NEAR, HEADS * WIDTH))),
        [SMEM] + [ANY] * 5,
        [pltpu.SemaphoreType.DMA((2, 3))],
        moved=4 << 20,
        places=(ANY, ANY),
    )(index, query_rows, key_rows, value_rows, out_grad, stats)
    core = partner(core, 1)
    chip = partner(chip, 2)
    relay = partner(chip, 1)
    far, pair = call(
        middle_kernel,
        "middle_rows",
        (shape((DEPTH, FAR, WIDTH)), shape((PAIR, WIDTH))),
        [SMEM, VMEM],
        [pltpu.VMEM((128, 128), F32)],
        moved=1 << 20,
    )(index, side)
    mine = far
    far = exchange(far, DEPTH_GROUPS)
    pair = partner(pair, 8)
    sums = call(
        pair_kernel,
        "pair_grads",
        shape((RING, OUT_CHUNK, WIDTH), F32),
        [SMEM, VMEM, VMEM],
        flops=2 * 10 * 128 * 256 * 256,
        moved=1 << 20,
    )(index, side, pair)
    plane = call(
        plane_kernel,
        "plane_rows",
        shape((ROWS, PLANE, WIDTH)),
        [SMEM, VMEM, ANY],
        moved=1 << 20,
    )(index, far, sums)
    near = shape(whole, F32)
    near_grads = call(
        near_kernel,
        "near_grads",
        (near, near, near),
        [SMEM] + [VMEM] * 8 + [ANY],
        flops=2 * 128 * 128 * 128 * 8 * 17,
        moved=6 << 20,
    )(index, query_rows, key_rows, value_rows, out_grad, stats, core, chip, relay, plane)
    plane = exchange(plane, ROW_GROUPS)
    grads = call(
        join_kernel,
        "join_grads",
        shape((RING, OUT_CHUNK, WIDTH)),
        [SMEM, VMEM, VMEM, VMEM, ANY],
        [pltpu.VMEM((RING, OUT_CHUNK, WIDTH), F32), pltpu.VMEM((128, 128), F32)],
        moved=1 << 20,
    )(index, plane, mine, sums, near_grads[0])
    grads = exchange(grads, RING_GROUPS)
    out = shape(whole)
    return call(
        post_kernel,
        "add_levels",
        (out, out, out),
        [VMEM] * 4,
        flops=2 * 128 * 32 * 3072,
        moved=4 << 20,
    )(grads, *near_grads)


def solution(mesh):
    return jax.shard_map(
        body,
        mesh=mesh,
        in_specs=(
            P("seq", None),
            P("seq", None),
            P("seq", None),
            P("seq", None),
            P("seq", None),
            P(None, "seq"),
        ),
        out_specs=(P("seq", None), P("seq", None), P("seq", None)),
        check_vma=False,
    )
```

```python
import functools

import jax
import jax.numpy as jnp
from jax import lax
from jax.experimental import pallas as pl
from jax.experimental.pallas import tpu as pltpu
from jax.sharding import PartitionSpec as P

HEADS = 8
WIDTH = 128
TOK = 128
RING = 8
DEPTH = 16
ROWS = 4
DEVICES = 512
SCALE = WIDTH**-0.5
SIDE = 32
CHUNK = 4 * SIDE + 16
OUT_CHUNK = 3 * SIDE
PAIR = 4 * 128 + 32
FAR = 40
PLANE = 2 * 128 + 16
NEAR = 2 * TOK + 16

BF = jnp.bfloat16
F32 = jnp.float32
VMEM = pl.BlockSpec(memory_space=pltpu.VMEM)
SMEM = pl.BlockSpec(memory_space=pltpu.SMEM)
ANY = pl.BlockSpec(memory_space=pl.ANY)


def iota(shape, dim):
    return lax.broadcasted_iota(jnp.int32, shape, dim)


def dot(a, b):
    return jnp.dot(a, b, preferred_element_type=F32)


def dot_nt(a, b):
    return lax.dot_general(a, b, (((1,), (1,)), ((), ())), preferred_element_type=F32)


def dot_tn(a, b):
    return lax.dot_general(a, b, (((0,), (0,)), ((), ())), preferred_element_type=F32)


def split3(x):
    high = x.astype(BF).astype(F32)
    rest = x - high
    middle = rest.astype(BF).astype(F32)
    low = (rest - middle).astype(BF).astype(F32)
    return high, middle, low


def place3(parts, slot, first):
    high, middle, low = parts
    return jnp.where(
        slot == first,
        high,
        jnp.where(slot == first + 1, middle, jnp.where(slot == first + 2, low, 0.0)),
    )


def columns_of(head):
    return slice(head * WIDTH, (head + 1) * WIDTH)


def stat_pair(tile):
    norm = tile[0:1] + tile[1:2] + tile[2:3]
    delta = tile[3:4] + tile[4:5] + tile[5:6]
    return norm, delta


def block_terms(query, key, value, grad, norm, delta, mask):
    scores = dot_nt(key, query) * SCALE
    probs = jnp.exp(scores - norm)
    if mask is not None:
        probs = jnp.where(mask, probs, 0.0)
    dprobs = dot_nt(value, grad)
    dscores = (probs * (dprobs - delta)).astype(BF)
    return probs.astype(BF), dscores


def select_kernel(i_ref, q_in, k_in, v_in, g_in, o_in, n_in, out_ref, stat_ref, q, k, v, g, o, n, sems):
    copies = [[pltpu.make_async_copy(n_in, n, sems.at[0, 0])]]
    for number, (source, place) in enumerate(
        ((g_in, g), (o_in, o), (q_in, q), (k_in, k), (v_in, v))
    ):
        copies.append(
            [
                pltpu.make_async_copy(
                    source.at[pl.ds(part * 64, 64)],
                    place.at[pl.ds(part * 64, 64)],
                    sems.at[number + 1, part],
                )
                for part in range(2)
            ]
        )
    for group in copies:
        for copy in group:
            copy.start()
    seat = i_ref[0] % RING
    for group in copies[0:3]:
        for copy in group:
            copy.wait()
    lane = iota((TOK, 128), 1)
    spread = jnp.zeros((TOK, 128), F32)
    for head in range(HEADS):
        product = g[:, columns_of(head)].astype(F32) * o[:, columns_of(head)].astype(F32)
        total = jnp.sum(product, axis=-1, keepdims=True)
        spread = jnp.where(lane // 16 == head, total, spread)
    deltas = place3(split3(spread), lane % 16, 3)
    norms = jnp.broadcast_to(n[...][:, None, :], (HEADS, 16, TOK)).reshape(128, TOK)
    norms = place3(split3(norms), iota((128, TOK), 0) % 16, 0)
    stats = (norms + deltas.T).astype(BF)
    for head in range(HEADS):
        stat_ref[:, columns_of(head)] = stats[head * 16 : (head + 1) * 16, :]
    token = iota((TOK, 128), 0)
    for residue in range(4):
        spot = ((token == 4 * (lane % SIDE) + residue) & (lane // SIDE == seat % 4)).astype(BF)
        placed = dot(stats, spot).astype(BF)
        for head in (residue, residue + 4):
            out_ref[head, 4 * SIDE : CHUNK, :] = placed[head * 16 : (head + 1) * 16, :]
    order = iota((TOK, TOK), 0)
    perm = (4 * (order % SIDE) + order // SIDE == iota((TOK, TOK), 1)).astype(BF)
    for tensor, (ref, group) in enumerate(
        ((q, copies[3]), (k, copies[4]), (v, copies[5]), (g, ()))
    ):
        for copy in group:
            copy.wait()
        ordered = dot(perm, ref[...]).astype(BF)
        for head in range(HEADS):
            start = SIDE * (head % 4)
            out_ref[head, tensor * SIDE : (tensor + 1) * SIDE, :] = ordered[
                start : start + SIDE, columns_of(head)
            ]


def payload_kernel(i_ref, q_in, k_in, v_in, g_in, s_in, core_ref, chip_ref, sems):
    index = i_ref[0]
    for number, (ref, bit) in enumerate(((core_ref, 1), (chip_ref, 2))):
        later = (index & bit) != 0

        def send(first, second, ref=ref, number=number):
            copies = [
                pltpu.make_async_copy(first, ref.at[pl.ds(0, TOK)], sems.at[number, 0]),
                pltpu.make_async_copy(second, ref.at[pl.ds(TOK, TOK)], sems.at[number, 1]),
                pltpu.make_async_copy(s_in, ref.at[pl.ds(2 * TOK, 16)], sems.at[number, 2]),
            ]
            for copy in copies:
                copy.start()
            for copy in copies:
                copy.wait()

        @pl.when(later)
        def _():
            send(q_in, g_in)

        @pl.when(jnp.logical_not(later))
        def _():
            send(k_in, v_in)


def near_kernel(i_ref, q, k, v, g, s, r1, r2, r3, after, out_ref):
    place = i_ref[0] % 4
    stat_rows = [stat_pair(s[:, columns_of(head)].astype(F32)) for head in range(HEADS)]
    stat_rows = [row[0] for row in stat_rows] + [row[1] for row in stat_rows]
    stat_columns = jnp.concatenate(stat_rows + [jnp.zeros((112, TOK), F32)], axis=0).T
    blocks = (r1, r2, r3)

    def part(block, number, c):
        return block[number * TOK : (TOK, 2 * TOK, NEAR)[number], c]

    def terms(earlier, later):
        for head in range(HEADS):
            c = columns_of(head)
            query, grad = q[:, c], g[:, c]
            key = jnp.concatenate([k[:, c]] + [part(block, 0, c) for block in earlier], axis=0)
            value = jnp.concatenate([v[:, c]] + [part(block, 1, c) for block in earlier], axis=0)
            size = key.shape[0]
            norm = stat_columns[:, head : head + 1]
            delta = stat_columns[:, HEADS + head : HEADS + head + 1]
            lane = iota((TOK, size), 1)
            mask = (lane <= iota((TOK, size), 0)) | (lane >= TOK)
            probs = jnp.where(mask, jnp.exp(dot_nt(query, key) * SCALE - norm), 0.0)
            dscores = (probs * (dot_nt(grad, value) - delta)).astype(BF)
            out_ref[0, :, c] = (dot(dscores, key) * SCALE).astype(BF)
            key_grad = dot_tn(dscores[:, 0:TOK], query)
            value_grad = dot_tn(probs[:, 0:TOK].astype(BF), grad)
            if later:
                query = jnp.concatenate([part(block, 0, c) for block in later], axis=0)
                grad = jnp.concatenate([part(block, 1, c) for block in later], axis=0)
                tile = jnp.concatenate([part(block, 2, c) for block in later], axis=1)
                norm, delta = stat_pair(tile.astype(F32))
                probs, dscores = block_terms(query, k[:, c], v[:, c], grad, norm, delta, None)
                key_grad = key_grad + dot(dscores, query)
                value_grad = value_grad + dot(probs, grad)
            out_ref[1, :, c] = (key_grad * SCALE).astype(BF)
            out_ref[2, :, c] = value_grad.astype(BF)

    cases = (
        ((), (0, 1, 2)),
        ((0,), (1, 2)),
        ((1, 2), (0,)),
        ((0, 1, 2), ()),
    )
    for number, (earlier, later) in enumerate(cases):

        @pl.when(place == number)
        def _(earlier=earlier, later=later):
            terms([blocks[i] for i in earlier], [blocks[i] for i in later])


def middle_kernel(i_ref, r_ref, far_ref, mine_ref, pair_ref, flat):
    index = i_ref[0]
    layer = (index // 8) % DEPTH
    place = index % RING
    upper = layer % 2 == 1
    lane = iota((16, 128), 1)
    tiles = [r_ref[s, 4 * SIDE : CHUNK, :].astype(F32) for s in range(RING)]
    stats = jnp.zeros((16, 128), F32)
    for s in range(RING):
        taken = jnp.where(lane == (s % 4) * SIDE + place // 4, tiles[s], 0.0)
        value = jnp.sum(taken, axis=1, keepdims=True)
        stats = jnp.where(lane == layer * RING + s, value, stats)
    rows = []
    for tensor in range(4):
        flat[...] = r_ref[:, tensor * SIDE : tensor * SIDE + 16, :].astype(F32).reshape(128, WIDTH)
        rows.append(flat[pl.ds(place // 4, RING, stride=16), :])
    payload = jnp.concatenate(rows + [stats[0:8]], axis=0).astype(BF)
    mine_ref[...] = payload
    for target in range(DEPTH):
        far_ref[target] = payload

    def fill(first, second):
        for number, tensor in enumerate((first, second)):
            pair_ref[number * 256 : (number + 1) * 256, :] = r_ref[
                :, tensor * SIDE : (tensor + 1) * SIDE, :
            ].reshape(256, WIDTH)

    @pl.when(upper)
    def _():
        fill(0, 3)

    @pl.when(jnp.logical_not(upper))
    def _():
        fill(1, 2)

    pair_ref[512:528, :] = (tiles[0] + tiles[1] + tiles[2] + tiles[3]).astype(BF)
    pair_ref[528:544, :] = (tiles[4] + tiles[5] + tiles[6] + tiles[7]).astype(BF)


def pair_kernel(i_ref, r_ref, x_ref, o_ref):
    upper = (i_ref[0] // 8) % 2 == 1

    def own(tensor):
        return r_ref[:, tensor * SIDE : (tensor + 1) * SIDE, :].reshape(256, WIDTH)

    def put(tensor, part):
        o_ref[:, tensor * SIDE : (tensor + 1) * SIDE, :] = part.reshape(RING, SIDE, WIDTH)

    def add(tensor, part):
        span = slice(tensor * SIDE, (tensor + 1) * SIDE)
        o_ref[:, span, :] = o_ref[:, span, :] + part.reshape(RING, SIDE, WIDTH)

    tiles = [r_ref[s, 4 * SIDE : CHUNK, :].astype(F32) for s in range(RING)]
    own_tile = jnp.concatenate(
        [tiles[0] + tiles[1] + tiles[2] + tiles[3], tiles[4] + tiles[5] + tiles[6] + tiles[7]],
        axis=1,
    )
    norm, delta = stat_pair(own_tile)
    query, key, value, grad = own(0), own(1), own(2), own(3)
    causal = iota((256, 256), 0) <= iota((256, 256), 1)
    probs, dscores = block_terms(query, key, value, grad, norm, delta, causal)
    put(0, dot_tn(dscores, key) * SCALE)
    put(1, dot(dscores, query) * SCALE)
    put(2, dot(probs, grad))

    @pl.when(upper)
    def _():
        far_key = x_ref[0:256, :]
        far_value = x_ref[256:512, :]
        _, dscores = block_terms(query, far_key, far_value, grad, norm, delta, None)
        add(0, dot_tn(dscores, far_key) * SCALE)

    @pl.when(jnp.logical_not(upper))
    def _():
        far_query = x_ref[0:256, :]
        far_grad = x_ref[256:512, :]
        far_tile = jnp.concatenate([x_ref[512:528, :], x_ref[528:544, :]], axis=1).astype(F32)
        far_norm, far_delta = stat_pair(far_tile)
        probs, dscores = block_terms(far_query, key, value, far_grad, far_norm, far_delta, None)
        add(1, dot(dscores, far_query) * SCALE)
        add(2, dot(probs, far_grad))


def plane_kernel(i_ref, r_ref, after_pair, o_ref):
    index = i_ref[0]
    row = index // 128
    layer = (index // 8) % DEPTH
    held = r_ref[...].astype(F32)
    query, key, value, grad = [
        held[:, tensor * 8 : (tensor + 1) * 8, :].reshape(128, WIDTH) for tensor in range(4)
    ]
    tile = jnp.sum(held[:, 32:FAR, :], axis=0)
    tile = jnp.concatenate([tile, jnp.zeros((8, 128), F32)], axis=0).astype(BF)
    depth = iota((128, WIDTH), 0) // RING
    for target in range(ROWS):
        cut = jnp.where(row < target, DEPTH, jnp.where(row == target, layer, 0))
        earlier = depth < cut
        o_ref[target, 0:128, :] = jnp.where(earlier, key, query).astype(BF)
        o_ref[target, 128:256, :] = jnp.where(earlier, value, grad).astype(BF)
        o_ref[target, 256:PLANE, :] = tile


def join_kernel(i_ref, f_ref, m_ref, n_ref, o_ref, sums, wide):
    index = i_ref[0]
    row = index // 128
    layer = (index // 8) % DEPTH
    place = index % RING
    here = row * DEPTH + layer
    sums[...] = n_ref[...]
    mine_all = m_ref[...].astype(F32)
    mine = [mine_all[tensor * 8 : (tensor + 1) * 8] for tensor in range(4)]
    stat_rows = [f_ref[y, 256:PLANE, :].astype(F32) for y in range(ROWS)]
    norm_row, delta_row = stat_pair(jnp.concatenate(stat_rows, axis=1))
    chosen = iota((8, 512), 1) == here * RING + iota((8, 512), 0)
    norm_column = jnp.sum(jnp.where(chosen, norm_row, 0.0), axis=1, keepdims=True)
    delta_column = jnp.sum(jnp.where(chosen, delta_row, 0.0), axis=1, keepdims=True)
    on_tail = iota((8, 128), 1) == 8 + iota((8, 128), 0)
    norm_tail = jnp.sum(jnp.where(on_tail, norm_column, 0.0), axis=0, keepdims=True)
    delta_tail = jnp.sum(jnp.where(on_tail, delta_column, 0.0), axis=0, keepdims=True)
    pad = jnp.zeros((112, WIDTH), F32)
    near_a = jnp.concatenate([mine[1], mine[0], pad], axis=0).astype(BF)
    near_b = jnp.concatenate([mine[2], mine[3], pad], axis=0).astype(BF)
    all_a = jnp.concatenate([f_ref[y, 0:128, :] for y in range(ROWS)] + [near_a], axis=0)
    all_b = jnp.concatenate([f_ref[y, 128:256, :] for y in range(ROWS)] + [near_b], axis=0)
    left = jnp.concatenate([mine[0], mine[1]], axis=0).astype(BF)
    right = jnp.concatenate([mine[3], mine[2]], axis=0).astype(BF)
    scores = dot_nt(left, all_a) * SCALE
    dprobs = dot_nt(right, all_b)
    norm_wide = jnp.concatenate([norm_row, norm_tail], axis=1)
    delta_wide = jnp.concatenate([delta_row, delta_tail], axis=1)
    norms = jnp.concatenate(
        [jnp.broadcast_to(norm_column, (8, 640)), jnp.broadcast_to(norm_wide, (8, 640))], axis=0
    )
    deltas = jnp.concatenate(
        [jnp.broadcast_to(delta_column, (8, 640)), jnp.broadcast_to(delta_wide, (8, 640))], axis=0
    )
    lane = iota((16, 640), 1)
    seat = iota((16, 640), 0)
    source = lane // RING
    tail = lane - 512
    low = jnp.where(lane < 512, source, jnp.where(tail < 8, here - 1 + (tail > seat), 1 << 20))
    high = jnp.where(
        lane < 512, source, jnp.where((tail >= 8) & (tail < 16), here + 1 - (tail < seat), -1)
    )
    valid = ((seat < 8) & (low < here)) | ((seat >= 8) & (high > here))
    probs = jnp.where(valid, jnp.exp(jnp.where(valid, scores - norms, 0.0)), 0.0)
    dscores = (probs * (dprobs - deltas)).astype(BF)
    wide[0:16, :] = dot(dscores, all_a) * SCALE
    wide[16:32, :] = dot(probs.astype(BF), all_b)
    for s in range(RING):
        for tensor, at in ((0, s), (1, 8 + s), (2, 24 + s)):
            span = pl.ds(tensor * SIDE + place // 4, 1)
            sums[s, span, :] = sums[s, span, :] + wide[at : at + 1, :]
    o_ref[...] = sums[...].astype(BF)


def post_kernel(r_ref, n_ref, q_ref, k_ref, v_ref):
    for tensor, ref in enumerate((q_ref, k_ref, v_ref)):
        for head in range(HEADS):
            residue = head % 4
            back = (iota((TOK, SIDE), 0) == 4 * iota((TOK, SIDE), 1) + residue).astype(BF)
            part = dot(back, r_ref[head, tensor * SIDE : (tensor + 1) * SIDE, :])
            ref[:, columns_of(head)] = (n_ref[tensor, :, columns_of(head)].astype(F32) + part).astype(BF)


def call(kernel, name, out, specs, scratch=(), flops=0, moved=0, places=None, limit=16):
    return pl.pallas_call(
        kernel,
        name=name,
        out_shape=out,
        in_specs=specs,
        out_specs=jax.tree.map(lambda _: VMEM, out) if places is None else places,
        scratch_shapes=list(scratch),
        cost_estimate=pl.CostEstimate(flops=flops, bytes_accessed=moved, transcendentals=0),
        compiler_params=pltpu.CompilerParams(vmem_limit_bytes=limit * 1024 * 1024),
    )


def shape(dims, dtype=BF):
    return jax.ShapeDtypeStruct(dims, dtype)


RING_GROUPS = [[base + i for i in range(RING)] for base in range(0, DEVICES, RING)]
DEPTH_GROUPS = [
    [y * 128 + z * 8 + i for z in range(DEPTH)] for y in range(ROWS) for i in range(RING)
]
ROW_GROUPS = [[y * 128 + i for y in range(ROWS)] for i in range(128)]


def exchange(array, groups):
    return lax.all_to_all(array, "seq", 0, 0, axis_index_groups=groups, tiled=True)


def partner(array, bit):
    return lax.ppermute(array, "seq", [(i, i ^ bit) for i in range(DEVICES)])


def body(query_rows, key_rows, value_rows, attn_out, out_grad, log_norms):
    index = lax.axis_index("seq").astype(jnp.int32).reshape(1)
    whole = (TOK, HEADS * WIDTH)
    side, stats = call(
        select_kernel,
        "select_rows",
        (shape((HEADS, CHUNK, WIDTH)), shape((16, HEADS * WIDTH))),
        [SMEM] + [ANY] * 6,
        [pltpu.VMEM(whole, BF)] * 5
        + [pltpu.VMEM((HEADS, TOK), F32), pltpu.SemaphoreType.DMA((6, 2))],
        flops=2 * 128 * 128 * 4096,
        moved=3 << 20,
        limit=60,
    )(index, query_rows, key_rows, value_rows, out_grad, attn_out, log_norms)
    side = exchange(side, RING_GROUPS)
    core, chip = call(
        payload_kernel,
        "near_payload",
        (shape((NEAR, HEADS * WIDTH)), shape((NEAR, HEADS * WIDTH))),
        [SMEM] + [ANY] * 5,
        [pltpu.SemaphoreType.DMA((2, 3))],
        moved=4 << 20,
        places=(ANY, ANY),
    )(index, query_rows, key_rows, value_rows, out_grad, stats)
    core = partner(core, 1)
    chip = partner(chip, 2)
    relay = partner(chip, 1)
    far, mine, pair = call(
        middle_kernel,
        "middle_rows",
        (shape((DEPTH, FAR, WIDTH)), shape((FAR, WIDTH)), shape((PAIR, WIDTH))),
        [SMEM, VMEM],
        [pltpu.VMEM((128, 128), F32)],
        moved=1 << 20,
    )(index, side)
    far = exchange(far, DEPTH_GROUPS)
    pair = partner(pair, 8)
    sums = call(
        pair_kernel,
        "pair_grads",
        shape((RING, OUT_CHUNK, WIDTH), F32),
        [SMEM, VMEM, VMEM],
        flops=8 * 2 * 10 * 128 * 256 * 256,
        moved=1 << 20,
    )(index, side, pair)
    plane = call(
        plane_kernel,
        "plane_rows",
        shape((ROWS, PLANE, WIDTH)),
        [SMEM, VMEM, ANY],
        moved=1 << 20,
    )(index, far, sums)
    plane = exchange(plane, ROW_GROUPS)
    grads = call(
        join_kernel,
        "join_grads",
        shape((RING, OUT_CHUNK, WIDTH)),
        [SMEM, VMEM, VMEM, VMEM],
        [pltpu.VMEM((RING, OUT_CHUNK, WIDTH), F32), pltpu.VMEM((128, 128), F32)],
        moved=1 << 20,
    )(index, plane, mine, sums)
    near_grads = call(
        near_kernel,
        "near_grads",
        shape((3, TOK, HEADS * WIDTH)),
        [SMEM] + [VMEM] * 8 + [ANY],
        flops=int(1 * 2 * 128 * 128 * 128 * 8 * 17),
        moved=4 << 20,
    )(index, query_rows, key_rows, value_rows, out_grad, stats, core, chip, relay, grads)
    grads = exchange(grads, RING_GROUPS)
    out = shape(whole)
    return call(
        post_kernel,
        "add_levels",
        (out, out, out),
        [VMEM] * 2,
        flops=2 * 128 * 32 * 3072,
        moved=4 << 20,
    )(grads, near_grads)


def solution(mesh):
    return jax.shard_map(
        body,
        mesh=mesh,
        in_specs=(
            P("seq", None),
            P("seq", None),
            P("seq", None),
            P("seq", None),
            P("seq", None),
            P(None, "seq"),
        ),
        out_specs=(P("seq", None), P("seq", None), P("seq", None)),
        check_vma=False,
    )
```

```python
import jax
import jax.numpy as jnp
from jax import lax
from jax.experimental import pallas as pl
from jax.experimental.pallas import tpu as pltpu
from jax.sharding import PartitionSpec as P

HEADS = 8
WIDTH = 128
TOK = 128
RING = 8
DEPTH = 16
ROWS = 4
DEVICES = 512
SCALE = WIDTH**-0.5
SIDE = 32
CHUNK = 4 * SIDE + 16
OUT_CHUNK = 3 * SIDE
PAIR = 4 * 128 + 32
FAR = 40
PLANE = 2 * 128 + 16
NEAR = 2 * TOK + 16

BF = jnp.bfloat16
F32 = jnp.float32
VMEM = pl.BlockSpec(memory_space=pltpu.VMEM)
SMEM = pl.BlockSpec(memory_space=pltpu.SMEM)
ANY = pl.BlockSpec(memory_space=pl.ANY)


def iota(shape, dim):
    return lax.broadcasted_iota(jnp.int32, shape, dim)


def dot(a, b):
    return jnp.dot(a, b, preferred_element_type=F32)


def dot_nt(a, b):
    return lax.dot_general(a, b, (((1,), (1,)), ((), ())), preferred_element_type=F32)


def dot_tn(a, b):
    return lax.dot_general(a, b, (((0,), (0,)), ((), ())), preferred_element_type=F32)


def split3(x):
    high = x.astype(BF).astype(F32)
    rest = x - high
    middle = rest.astype(BF).astype(F32)
    low = (rest - middle).astype(BF).astype(F32)
    return high, middle, low


def place3(parts, slot, first):
    high, middle, low = parts
    return jnp.where(
        slot == first,
        high,
        jnp.where(slot == first + 1, middle, jnp.where(slot == first + 2, low, 0.0)),
    )


def columns_of(head):
    return slice(head * WIDTH, (head + 1) * WIDTH)


def stat_pair(tile):
    norm = tile[0:1] + tile[1:2] + tile[2:3]
    delta = tile[3:4] + tile[4:5] + tile[5:6]
    return norm, delta


def block_terms(query, key, value, grad, norm, delta, mask):
    scores = dot_nt(key, query) * SCALE
    probs = jnp.exp(scores - norm)
    if mask is not None:
        probs = jnp.where(mask, probs, 0.0)
    dprobs = dot_nt(value, grad)
    dscores = (probs * (dprobs - delta)).astype(BF)
    return probs.astype(BF), dscores


def select_kernel(i_ref, q_in, k_in, v_in, g_in, o_in, n_in, out_ref, stat_ref, q, k, v, g, o, n, sems):
    copies = [[pltpu.make_async_copy(n_in, n, sems.at[0, 0])]]
    for number, (source, place) in enumerate(
        ((g_in, g), (o_in, o), (q_in, q), (k_in, k), (v_in, v))
    ):
        copies.append(
            [
                pltpu.make_async_copy(
                    source.at[pl.ds(part * 64, 64)],
                    place.at[pl.ds(part * 64, 64)],
                    sems.at[number + 1, part],
                )
                for part in range(2)
            ]
        )
    for group in copies:
        for copy in group:
            copy.start()
    seat = i_ref[0] % RING
    for group in copies[0:3]:
        for copy in group:
            copy.wait()
    lane = iota((TOK, 128), 1)
    spread = jnp.zeros((TOK, 128), F32)
    for head in range(HEADS):
        product = g[:, columns_of(head)].astype(F32) * o[:, columns_of(head)].astype(F32)
        total = jnp.sum(product, axis=-1, keepdims=True)
        spread = jnp.where(lane // 16 == head, total, spread)
    deltas = place3(split3(spread), lane % 16, 3)
    norms = jnp.broadcast_to(n[...][:, None, :], (HEADS, 16, TOK)).reshape(128, TOK)
    norms = place3(split3(norms), iota((128, TOK), 0) % 16, 0)
    stats = (norms + deltas.T).astype(BF)
    for head in range(HEADS):
        stat_ref[:, columns_of(head)] = stats[head * 16 : (head + 1) * 16, :]
    token = iota((TOK, 128), 0)
    for residue in range(4):
        spot = ((token == 4 * (lane % SIDE) + residue) & (lane // SIDE == seat % 4)).astype(BF)
        placed = dot(stats, spot).astype(BF)
        for head in (residue, residue + 4):
            out_ref[head, 4 * SIDE : CHUNK, :] = placed[head * 16 : (head + 1) * 16, :]
    order = iota((TOK, TOK), 0)
    perm = (4 * (order % SIDE) + order // SIDE == iota((TOK, TOK), 1)).astype(BF)
    for tensor, (ref, group) in enumerate(
        ((q, copies[3]), (k, copies[4]), (v, copies[5]), (g, ()))
    ):
        for copy in group:
            copy.wait()
        ordered = dot(perm, ref[...]).astype(BF)
        for head in range(HEADS):
            start = SIDE * (head % 4)
            out_ref[head, tensor * SIDE : (tensor + 1) * SIDE, :] = ordered[
                start : start + SIDE, columns_of(head)
            ]


def payload_kernel(i_ref, q_in, k_in, v_in, g_in, s_in, core_ref, chip_ref, sems):
    index = i_ref[0]
    for number, (ref, bit) in enumerate(((core_ref, 1), (chip_ref, 2))):
        later = (index & bit) != 0

        def send(first, second, ref=ref, number=number):
            copies = [
                pltpu.make_async_copy(first, ref.at[pl.ds(0, TOK)], sems.at[number, 0]),
                pltpu.make_async_copy(second, ref.at[pl.ds(TOK, TOK)], sems.at[number, 1]),
                pltpu.make_async_copy(s_in, ref.at[pl.ds(2 * TOK, 16)], sems.at[number, 2]),
            ]
            for copy in copies:
                copy.start()
            for copy in copies:
                copy.wait()

        @pl.when(later)
        def _():
            send(q_in, g_in)

        @pl.when(jnp.logical_not(later))
        def _():
            send(k_in, v_in)


def near_kernel(i_ref, q, k, v, g, s, r1, r2, r3, after, out_ref):
    place = i_ref[0] % 4
    stat_rows = [stat_pair(s[:, columns_of(head)].astype(F32)) for head in range(HEADS)]
    stat_rows = [row[0] for row in stat_rows] + [row[1] for row in stat_rows]
    stat_columns = jnp.concatenate(stat_rows + [jnp.zeros((112, TOK), F32)], axis=0).T
    blocks = (r1, r2, r3)

    def part(block, number, c):
        return block[number * TOK : (TOK, 2 * TOK, NEAR)[number], c]

    def terms(earlier, later):
        for head in range(HEADS):
            c = columns_of(head)
            query, grad = q[:, c], g[:, c]
            key = jnp.concatenate([k[:, c]] + [part(block, 0, c) for block in earlier], axis=0)
            value = jnp.concatenate([v[:, c]] + [part(block, 1, c) for block in earlier], axis=0)
            size = key.shape[0]
            norm = stat_columns[:, head : head + 1]
            delta = stat_columns[:, HEADS + head : HEADS + head + 1]
            lane = iota((TOK, size), 1)
            mask = (lane <= iota((TOK, size), 0)) | (lane >= TOK)
            probs = jnp.where(mask, jnp.exp(dot_nt(query, key) * SCALE - norm), 0.0)
            dscores = (probs * (dot_nt(grad, value) - delta)).astype(BF)
            out_ref[0, :, c] = (dot(dscores, key) * SCALE).astype(BF)
            key_grad = dot_tn(dscores[:, 0:TOK], query)
            value_grad = dot_tn(probs[:, 0:TOK].astype(BF), grad)
            if later:
                query = jnp.concatenate([part(block, 0, c) for block in later], axis=0)
                grad = jnp.concatenate([part(block, 1, c) for block in later], axis=0)
                tile = jnp.concatenate([part(block, 2, c) for block in later], axis=1)
                norm, delta = stat_pair(tile.astype(F32))
                probs, dscores = block_terms(query, k[:, c], v[:, c], grad, norm, delta, None)
                key_grad = key_grad + dot(dscores, query)
                value_grad = value_grad + dot(probs, grad)
            out_ref[1, :, c] = (key_grad * SCALE).astype(BF)
            out_ref[2, :, c] = value_grad.astype(BF)

    cases = (
        ((), (0, 1, 2)),
        ((0,), (1, 2)),
        ((1, 2), (0,)),
        ((0, 1, 2), ()),
    )
    for number, (earlier, later) in enumerate(cases):

        @pl.when(place == number)
        def _(earlier=earlier, later=later):
            terms([blocks[i] for i in earlier], [blocks[i] for i in later])


def middle_kernel(i_ref, r_ref, far_ref, mine_ref, pair_ref, flat):
    index = i_ref[0]
    layer = (index // 8) % DEPTH
    place = index % RING
    upper = layer % 2 == 1
    lane = iota((16, 128), 1)
    tiles = [r_ref[s, 4 * SIDE : CHUNK, :].astype(F32) for s in range(RING)]
    stats = jnp.zeros((16, 128), F32)
    for s in range(RING):
        taken = jnp.where(lane == (s % 4) * SIDE + place // 4, tiles[s], 0.0)
        value = jnp.sum(taken, axis=1, keepdims=True)
        stats = jnp.where(lane == layer * RING + s, value, stats)
    rows = []
    for tensor in range(4):
        first = tensor * SIDE
        flat[0:128] = r_ref[:, first : first + 16, :].astype(F32).reshape(128, WIDTH)
        rows.append(flat[pl.ds(place // 4, RING, stride=16), :])
    payload = jnp.concatenate(rows + [stats[0:8]], axis=0).astype(BF)
    mine_ref[...] = payload
    for target in range(DEPTH):
        far_ref[target] = payload

    def fill(first, second):
        for number, tensor in enumerate((first, second)):
            pair_ref[number * 256 : (number + 1) * 256, :] = r_ref[
                :, tensor * SIDE : (tensor + 1) * SIDE, :
            ].reshape(256, WIDTH)

    @pl.when(upper)
    def _():
        fill(0, 3)

    @pl.when(jnp.logical_not(upper))
    def _():
        fill(1, 2)

    pair_ref[512:528, :] = (tiles[0] + tiles[1] + tiles[2] + tiles[3]).astype(BF)
    pair_ref[528:544, :] = (tiles[4] + tiles[5] + tiles[6] + tiles[7]).astype(BF)


def pair_kernel(i_ref, r_ref, x_ref, o_ref):
    upper = (i_ref[0] // 8) % 2 == 1

    def own(tensor):
        return r_ref[:, tensor * SIDE : (tensor + 1) * SIDE, :].reshape(256, WIDTH)

    def put(tensor, part):
        o_ref[:, tensor * SIDE : (tensor + 1) * SIDE, :] = part.reshape(RING, SIDE, WIDTH)

    def add(tensor, part):
        span = slice(tensor * SIDE, (tensor + 1) * SIDE)
        o_ref[:, span, :] = o_ref[:, span, :] + part.reshape(RING, SIDE, WIDTH)

    tiles = [r_ref[s, 4 * SIDE : CHUNK, :].astype(F32) for s in range(RING)]
    own_tile = jnp.concatenate(
        [tiles[0] + tiles[1] + tiles[2] + tiles[3], tiles[4] + tiles[5] + tiles[6] + tiles[7]],
        axis=1,
    )
    norm, delta = stat_pair(own_tile)
    query, key, value, grad = own(0), own(1), own(2), own(3)
    causal = iota((256, 256), 0) <= iota((256, 256), 1)
    probs, dscores = block_terms(query, key, value, grad, norm, delta, causal)
    put(0, dot_tn(dscores, key) * SCALE)
    put(1, dot(dscores, query) * SCALE)
    put(2, dot(probs, grad))

    @pl.when(upper)
    def _():
        far_key = x_ref[0:256, :]
        far_value = x_ref[256:512, :]
        _, dscores = block_terms(query, far_key, far_value, grad, norm, delta, None)
        add(0, dot_tn(dscores, far_key) * SCALE)

    @pl.when(jnp.logical_not(upper))
    def _():
        far_query = x_ref[0:256, :]
        far_grad = x_ref[256:512, :]
        far_tile = jnp.concatenate([x_ref[512:528, :], x_ref[528:544, :]], axis=1).astype(F32)
        far_norm, far_delta = stat_pair(far_tile)
        probs, dscores = block_terms(far_query, key, value, far_grad, far_norm, far_delta, None)
        add(1, dot(dscores, far_query) * SCALE)
        add(2, dot(probs, far_grad))


def plane_kernel(i_ref, r_ref, after_pair, o_ref):
    index = i_ref[0]
    row = index // 128
    layer = (index // 8) % DEPTH
    held = r_ref[...].astype(F32)
    query, key, value, grad = [
        held[:, tensor * 8 : (tensor + 1) * 8, :].reshape(128, WIDTH) for tensor in range(4)
    ]
    tile = jnp.sum(held[:, 32:FAR, :], axis=0)
    tile = jnp.concatenate([tile, jnp.zeros((8, 128), F32)], axis=0).astype(BF)
    depth = iota((128, WIDTH), 0) // RING
    for target in range(ROWS):
        cut = jnp.where(row < target, DEPTH, jnp.where(row == target, layer, 0))
        earlier = depth < cut
        o_ref[target, 0:128, :] = jnp.where(earlier, key, query).astype(BF)
        o_ref[target, 128:256, :] = jnp.where(earlier, value, grad).astype(BF)
        o_ref[target, 256:PLANE, :] = tile


def join_kernel(i_ref, f_ref, m_ref, n_ref, o_ref, sums, wide):
    index = i_ref[0]
    row = index // 128
    layer = (index // 8) % DEPTH
    place = index % RING
    here = row * DEPTH + layer
    sums[...] = n_ref[...]
    mine_all = m_ref[...].astype(F32)
    mine = [mine_all[tensor * 8 : (tensor + 1) * 8] for tensor in range(4)]
    stat_rows = [f_ref[y, 256:PLANE, :].astype(F32) for y in range(ROWS)]
    norm_row, delta_row = stat_pair(jnp.concatenate(stat_rows, axis=1))
    chosen = iota((8, 512), 1) == here * RING + iota((8, 512), 0)
    norm_column = jnp.sum(jnp.where(chosen, norm_row, 0.0), axis=1, keepdims=True)
    delta_column = jnp.sum(jnp.where(chosen, delta_row, 0.0), axis=1, keepdims=True)
    on_tail = iota((8, 128), 1) == 8 + iota((8, 128), 0)
    norm_tail = jnp.sum(jnp.where(on_tail, norm_column, 0.0), axis=0, keepdims=True)
    delta_tail = jnp.sum(jnp.where(on_tail, delta_column, 0.0), axis=0, keepdims=True)
    pad = jnp.zeros((112, WIDTH), F32)
    near_a = jnp.concatenate([mine[1], mine[0], pad], axis=0).astype(BF)
    near_b = jnp.concatenate([mine[2], mine[3], pad], axis=0).astype(BF)
    all_a = jnp.concatenate([f_ref[y, 0:128, :] for y in range(ROWS)] + [near_a], axis=0)
    all_b = jnp.concatenate([f_ref[y, 128:256, :] for y in range(ROWS)] + [near_b], axis=0)
    left = jnp.concatenate([mine[0], mine[1]], axis=0).astype(BF)
    right = jnp.concatenate([mine[3], mine[2]], axis=0).astype(BF)
    scores = dot_nt(left, all_a) * SCALE
    dprobs = dot_nt(right, all_b)
    norm_wide = jnp.concatenate([norm_row, norm_tail], axis=1)
    delta_wide = jnp.concatenate([delta_row, delta_tail], axis=1)
    norms = jnp.concatenate(
        [jnp.broadcast_to(norm_column, (8, 640)), jnp.broadcast_to(norm_wide, (8, 640))], axis=0
    )
    deltas = jnp.concatenate(
        [jnp.broadcast_to(delta_column, (8, 640)), jnp.broadcast_to(delta_wide, (8, 640))], axis=0
    )
    lane = iota((16, 640), 1)
    seat = iota((16, 640), 0)
    source = lane // RING
    tail = lane - 512
    low = jnp.where(lane < 512, source, jnp.where(tail < 8, here - 1 + (tail > seat), 1 << 20))
    high = jnp.where(
        lane < 512, source, jnp.where((tail >= 8) & (tail < 16), here + 1 - (tail < seat), -1)
    )
    valid = ((seat < 8) & (low < here)) | ((seat >= 8) & (high > here))
    probs = jnp.where(valid, jnp.exp(jnp.where(valid, scores - norms, 0.0)), 0.0)
    dscores = (probs * (dprobs - deltas)).astype(BF)
    wide[0:16, :] = dot(dscores, all_a) * SCALE
    wide[16:32, :] = dot(probs.astype(BF), all_b)
    for s in range(RING):
        for tensor, at in ((0, s), (1, 8 + s), (2, 24 + s)):
            span = pl.ds(tensor * SIDE + place // 4, 1)
            sums[s, span, :] = sums[s, span, :] + wide[at : at + 1, :]
    o_ref[...] = sums[...].astype(BF)


def post_kernel(r_ref, n_ref, q_ref, k_ref, v_ref):
    for tensor, ref in enumerate((q_ref, k_ref, v_ref)):
        for head in range(HEADS):
            residue = head % 4
            back = (iota((TOK, SIDE), 0) == 4 * iota((TOK, SIDE), 1) + residue).astype(BF)
            part = dot(back, r_ref[head, tensor * SIDE : (tensor + 1) * SIDE, :])
            ref[:, columns_of(head)] = (n_ref[tensor, :, columns_of(head)].astype(F32) + part).astype(BF)


def call(kernel, name, out, specs, scratch=(), flops=0, moved=0, places=None, limit=16):
    return pl.pallas_call(
        kernel,
        name=name,
        out_shape=out,
        in_specs=specs,
        out_specs=jax.tree.map(lambda _: VMEM, out) if places is None else places,
        scratch_shapes=list(scratch),
        cost_estimate=pl.CostEstimate(flops=flops, bytes_accessed=moved, transcendentals=0),
        compiler_params=pltpu.CompilerParams(vmem_limit_bytes=limit * 1024 * 1024),
    )


def shape(dims, dtype=BF):
    return jax.ShapeDtypeStruct(dims, dtype)


RING_GROUPS = [[base + i for i in range(RING)] for base in range(0, DEVICES, RING)]
DEPTH_GROUPS = [
    [y * 128 + z * 8 + i for z in range(DEPTH)] for y in range(ROWS) for i in range(RING)
]
ROW_GROUPS = [[y * 128 + i for y in range(ROWS)] for i in range(128)]


def exchange(array, groups):
    return lax.all_to_all(array, "seq", 0, 0, axis_index_groups=groups, tiled=True)


def partner(array, bit):
    return lax.ppermute(array, "seq", [(i, i ^ bit) for i in range(DEVICES)])


def body(query_rows, key_rows, value_rows, attn_out, out_grad, log_norms):
    index = lax.axis_index("seq").astype(jnp.int32).reshape(1)
    whole = (TOK, HEADS * WIDTH)
    side, stats = call(
        select_kernel,
        "select_rows",
        (shape((HEADS, CHUNK, WIDTH)), shape((16, HEADS * WIDTH))),
        [SMEM] + [ANY] * 6,
        [pltpu.VMEM(whole, BF)] * 5
        + [pltpu.VMEM((HEADS, TOK), F32), pltpu.SemaphoreType.DMA((6, 2))],
        flops=2 * 128 * 128 * 4096,
        moved=3 << 20,
        limit=60,
    )(index, query_rows, key_rows, value_rows, out_grad, attn_out, log_norms)
    side = exchange(side, RING_GROUPS)
    core, chip = call(
        payload_kernel,
        "near_payload",
        (shape((NEAR, HEADS * WIDTH)), shape((NEAR, HEADS * WIDTH))),
        [SMEM] + [ANY] * 5,
        [pltpu.SemaphoreType.DMA((2, 3))],
        moved=4 << 20,
        places=(ANY, ANY),
    )(index, query_rows, key_rows, value_rows, out_grad, stats)
    core = partner(core, 1)
    chip = partner(chip, 2)
    relay = partner(chip, 1)
    far, mine, pair = call(
        middle_kernel,
        "middle_rows",
        (shape((DEPTH, FAR, WIDTH)), shape((FAR, WIDTH)), shape((PAIR, WIDTH))),
        [SMEM, VMEM],
        [pltpu.VMEM((144, 128), F32)],
        moved=1 << 20,
    )(index, side)
    far = exchange(far, DEPTH_GROUPS)
    pair = partner(pair, 8)
    sums = call(
        pair_kernel,
        "pair_grads",
        shape((RING, OUT_CHUNK, WIDTH), F32),
        [SMEM, VMEM, VMEM],
        flops=8 * 2 * 10 * 128 * 256 * 256,
        moved=1 << 20,
    )(index, side, pair)
    plane = call(
        plane_kernel,
        "plane_rows",
        shape((ROWS, PLANE, WIDTH)),
        [SMEM, VMEM, ANY],
        moved=1 << 20,
    )(index, far, sums)
    plane = exchange(plane, ROW_GROUPS)
    grads = call(
        join_kernel,
        "join_grads",
        shape((RING, OUT_CHUNK, WIDTH)),
        [SMEM, VMEM, VMEM, VMEM],
        [pltpu.VMEM((RING, OUT_CHUNK, WIDTH), F32), pltpu.VMEM((128, 128), F32)],
        moved=1 << 20,
    )(index, plane, mine, sums)
    near_grads = call(
        near_kernel,
        "near_grads",
        shape((3, TOK, HEADS * WIDTH)),
        [SMEM] + [VMEM] * 8 + [ANY],
        flops=int(1 * 2 * 128 * 128 * 128 * 8 * 17),
        moved=4 << 20,
    )(index, query_rows, key_rows, value_rows, out_grad, stats, core, chip, relay, grads)
    grads = exchange(grads, RING_GROUPS)
    out = shape(whole)
    return call(
        post_kernel,
        "add_levels",
        (out, out, out),
        [VMEM] * 2,
        flops=2 * 128 * 32 * 3072,
        moved=4 << 20,
    )(grads, near_grads)


def solution(mesh):
    return jax.shard_map(
        body,
        mesh=mesh,
        in_specs=(
            P("seq", None),
            P("seq", None),
            P("seq", None),
            P("seq", None),
            P("seq", None),
            P(None, "seq"),
        ),
        out_specs=(P("seq", None), P("seq", None), P("seq", None)),
        check_vma=False,
    )
```

```python
import jax
import jax.numpy as jnp
from jax import lax
from jax.experimental import pallas as pl
from jax.experimental.pallas import tpu as pltpu
from jax.sharding import PartitionSpec as P

HEADS = 8
WIDTH = 128
TOK = 128
RING = 8
DEPTH = 16
ROWS = 4
DEVICES = 512
SCALE = WIDTH**-0.5
SIDE = 32
CHUNK = 4 * SIDE + 16
OUT_CHUNK = 3 * SIDE
PAIR = 4 * 128 + 32
FAR = 40
PLANE = 2 * 128 + 16
NEAR = 2 * TOK + 16

BF = jnp.bfloat16
F32 = jnp.float32
VMEM = pl.BlockSpec(memory_space=pltpu.VMEM)
SMEM = pl.BlockSpec(memory_space=pltpu.SMEM)
ANY = pl.BlockSpec(memory_space=pl.ANY)


def iota(shape, dim):
    return lax.broadcasted_iota(jnp.int32, shape, dim)


def dot(a, b):
    return jnp.dot(a, b, preferred_element_type=F32)


def dot_nt(a, b):
    return lax.dot_general(a, b, (((1,), (1,)), ((), ())), preferred_element_type=F32)


def dot_tn(a, b):
    return lax.dot_general(a, b, (((0,), (0,)), ((), ())), preferred_element_type=F32)


def split3(x):
    high = x.astype(BF).astype(F32)
    rest = x - high
    middle = rest.astype(BF).astype(F32)
    low = (rest - middle).astype(BF).astype(F32)
    return high, middle, low


def place3(parts, slot, first):
    high, middle, low = parts
    return jnp.where(
        slot == first,
        high,
        jnp.where(slot == first + 1, middle, jnp.where(slot == first + 2, low, 0.0)),
    )


def columns_of(head):
    return slice(head * WIDTH, (head + 1) * WIDTH)


def stat_pair(tile):
    norm = tile[0:1] + tile[1:2] + tile[2:3]
    delta = tile[3:4] + tile[4:5] + tile[5:6]
    return norm, delta


def block_terms(query, key, value, grad, norm, delta, mask):
    scores = dot_nt(key, query) * SCALE
    probs = jnp.exp(scores - norm)
    if mask is not None:
        probs = jnp.where(mask, probs, 0.0)
    dprobs = dot_nt(value, grad)
    dscores = (probs * (dprobs - delta)).astype(BF)
    return probs.astype(BF), dscores


def select_kernel(i_ref, q_in, k_in, v_in, g_in, o_in, n_in, out_ref, stat_ref, q, k, v, g, o, n, sems):
    copies = [[pltpu.make_async_copy(n_in, n, sems.at[0, 0])]]
    for number, (source, place) in enumerate(
        ((g_in, g), (o_in, o), (q_in, q), (k_in, k), (v_in, v))
    ):
        copies.append(
            [
                pltpu.make_async_copy(
                    source.at[pl.ds(part * 64, 64)],
                    place.at[pl.ds(part * 64, 64)],
                    sems.at[number + 1, part],
                )
                for part in range(2)
            ]
        )
    for group in copies:
        for copy in group:
            copy.start()
    seat = i_ref[0] % RING
    for group in copies[0:3]:
        for copy in group:
            copy.wait()
    lane = iota((TOK, 128), 1)
    spread = jnp.zeros((TOK, 128), F32)
    for head in range(HEADS):
        product = g[:, columns_of(head)].astype(F32) * o[:, columns_of(head)].astype(F32)
        total = jnp.sum(product, axis=-1, keepdims=True)
        spread = jnp.where(lane // 16 == head, total, spread)
    deltas = place3(split3(spread), lane % 16, 3)
    norms = jnp.broadcast_to(n[...][:, None, :], (HEADS, 16, TOK)).reshape(128, TOK)
    norms = place3(split3(norms), iota((128, TOK), 0) % 16, 0)
    stats = (norms + deltas.T).astype(BF)
    for head in range(HEADS):
        stat_ref[:, columns_of(head)] = stats[head * 16 : (head + 1) * 16, :]
    token = iota((TOK, 128), 0)
    for residue in range(4):
        spot = ((token == 4 * (lane % SIDE) + residue) & (lane // SIDE == seat % 4)).astype(BF)
        placed = dot(stats, spot).astype(BF)
        for head in (residue, residue + 4):
            out_ref[head, 4 * SIDE : CHUNK, :] = placed[head * 16 : (head + 1) * 16, :]
    order = iota((TOK, TOK), 0)
    perm = (4 * (order % SIDE) + order // SIDE == iota((TOK, TOK), 1)).astype(BF)
    for tensor, (ref, group) in enumerate(
        ((q, copies[3]), (k, copies[4]), (v, copies[5]), (g, ()))
    ):
        for copy in group:
            copy.wait()
        ordered = dot(perm, ref[...]).astype(BF)
        for head in range(HEADS):
            start = SIDE * (head % 4)
            out_ref[head, tensor * SIDE : (tensor + 1) * SIDE, :] = ordered[
                start : start + SIDE, columns_of(head)
            ]


def payload_kernel(i_ref, q_in, k_in, v_in, g_in, s_in, core_ref, chip_ref, sems):
    index = i_ref[0]
    for number, (ref, bit) in enumerate(((core_ref, 1), (chip_ref, 2))):
        later = (index & bit) != 0

        def send(first, second, ref=ref, number=number):
            copies = [
                pltpu.make_async_copy(first, ref.at[pl.ds(0, TOK)], sems.at[number, 0]),
                pltpu.make_async_copy(second, ref.at[pl.ds(TOK, TOK)], sems.at[number, 1]),
                pltpu.make_async_copy(s_in, ref.at[pl.ds(2 * TOK, 16)], sems.at[number, 2]),
            ]
            for copy in copies:
                copy.start()
            for copy in copies:
                copy.wait()

        @pl.when(later)
        def _():
            send(q_in, g_in)

        @pl.when(jnp.logical_not(later))
        def _():
            send(k_in, v_in)


def near_kernel(i_ref, q, k, v, g, s, r1, r2, r3, after, out_ref):
    place = i_ref[0] % 4
    stat_rows = [stat_pair(s[:, columns_of(head)].astype(F32)) for head in range(HEADS)]
    stat_rows = [row[0] for row in stat_rows] + [row[1] for row in stat_rows]
    stat_columns = jnp.concatenate(stat_rows + [jnp.zeros((112, TOK), F32)], axis=0).T
    blocks = (r1, r2, r3)

    def part(block, number, c):
        return block[number * TOK : (TOK, 2 * TOK, NEAR)[number], c]

    def terms(earlier, later):
        for head in range(HEADS):
            c = columns_of(head)
            query, grad = q[:, c], g[:, c]
            key = jnp.concatenate([k[:, c]] + [part(block, 0, c) for block in earlier], axis=0)
            value = jnp.concatenate([v[:, c]] + [part(block, 1, c) for block in earlier], axis=0)
            size = key.shape[0]
            norm = stat_columns[:, head : head + 1]
            delta = stat_columns[:, HEADS + head : HEADS + head + 1]
            lane = iota((TOK, size), 1)
            mask = (lane <= iota((TOK, size), 0)) | (lane >= TOK)
            probs = jnp.where(mask, jnp.exp(dot_nt(query, key) * SCALE - norm), 0.0)
            dscores = (probs * (dot_nt(grad, value) - delta)).astype(BF)
            out_ref[0, :, c] = (dot(dscores, key) * SCALE).astype(BF)
            key_grad = dot_tn(dscores[:, 0:TOK], query)
            value_grad = dot_tn(probs[:, 0:TOK].astype(BF), grad)
            if later:
                query = jnp.concatenate([part(block, 0, c) for block in later], axis=0)
                grad = jnp.concatenate([part(block, 1, c) for block in later], axis=0)
                tile = jnp.concatenate([part(block, 2, c) for block in later], axis=1)
                norm, delta = stat_pair(tile.astype(F32))
                probs, dscores = block_terms(query, k[:, c], v[:, c], grad, norm, delta, None)
                key_grad = key_grad + dot(dscores, query)
                value_grad = value_grad + dot(probs, grad)
            out_ref[1, :, c] = (key_grad * SCALE).astype(BF)
            out_ref[2, :, c] = value_grad.astype(BF)

    cases = (
        ((), (0, 1, 2)),
        ((0,), (1, 2)),
        ((1, 2), (0,)),
        ((0, 1, 2), ()),
    )
    for number, (earlier, later) in enumerate(cases):

        @pl.when(place == number)
        def _(earlier=earlier, later=later):
            terms([blocks[i] for i in earlier], [blocks[i] for i in later])


def middle_kernel(i_ref, r_ref, far_ref, mine_ref, pair_ref, flat):
    index = i_ref[0]
    layer = (index // 8) % DEPTH
    place = index % RING
    upper = layer % 2 == 1
    lane = iota((16, 128), 1)
    tiles = [r_ref[s, 4 * SIDE : CHUNK, :].astype(F32) for s in range(RING)]
    stats = jnp.zeros((16, 128), F32)
    for s in range(RING):
        taken = jnp.where(lane == (s % 4) * SIDE + place // 4, tiles[s], 0.0)
        value = jnp.sum(taken, axis=1, keepdims=True)
        stats = jnp.where(lane == layer * RING + s, value, stats)
    rows = []
    for tensor in range(4):
        first = tensor * SIDE
        flat[0:128] = r_ref[:, first : first + 16, :].astype(F32).reshape(128, WIDTH)
        rows.append(flat[pl.ds(place // 4, RING, stride=16), :])
    payload = jnp.concatenate(rows + [stats[0:8]], axis=0).astype(BF)
    mine_ref[...] = payload
    for target in range(DEPTH):
        far_ref[target] = payload

    def fill(first, second):
        for number, tensor in enumerate((first, second)):
            pair_ref[number * 256 : (number + 1) * 256, :] = r_ref[
                :, tensor * SIDE : (tensor + 1) * SIDE, :
            ].reshape(256, WIDTH)

    @pl.when(upper)
    def _():
        fill(0, 3)

    @pl.when(jnp.logical_not(upper))
    def _():
        fill(1, 2)

    pair_ref[512:528, :] = (tiles[0] + tiles[1] + tiles[2] + tiles[3]).astype(BF)
    pair_ref[528:544, :] = (tiles[4] + tiles[5] + tiles[6] + tiles[7]).astype(BF)


def pair_kernel(i_ref, r_ref, x_ref, after, o_ref):
    upper = (i_ref[0] // 8) % 2 == 1

    def own(tensor):
        return r_ref[:, tensor * SIDE : (tensor + 1) * SIDE, :].reshape(256, WIDTH)

    def put(tensor, part):
        o_ref[:, tensor * SIDE : (tensor + 1) * SIDE, :] = part.reshape(RING, SIDE, WIDTH)

    def add(tensor, part):
        span = slice(tensor * SIDE, (tensor + 1) * SIDE)
        o_ref[:, span, :] = o_ref[:, span, :] + part.reshape(RING, SIDE, WIDTH)

    tiles = [r_ref[s, 4 * SIDE : CHUNK, :].astype(F32) for s in range(RING)]
    own_tile = jnp.concatenate(
        [tiles[0] + tiles[1] + tiles[2] + tiles[3], tiles[4] + tiles[5] + tiles[6] + tiles[7]],
        axis=1,
    )
    norm, delta = stat_pair(own_tile)
    query, key, value, grad = own(0), own(1), own(2), own(3)
    causal = iota((256, 256), 0) <= iota((256, 256), 1)
    probs, dscores = block_terms(query, key, value, grad, norm, delta, causal)
    put(0, dot_tn(dscores, key) * SCALE)
    put(1, dot(dscores, query) * SCALE)
    put(2, dot(probs, grad))

    @pl.when(upper)
    def _():
        far_key = x_ref[0:256, :]
        far_value = x_ref[256:512, :]
        _, dscores = block_terms(query, far_key, far_value, grad, norm, delta, None)
        add(0, dot_tn(dscores, far_key) * SCALE)

    @pl.when(jnp.logical_not(upper))
    def _():
        far_query = x_ref[0:256, :]
        far_grad = x_ref[256:512, :]
        far_tile = jnp.concatenate([x_ref[512:528, :], x_ref[528:544, :]], axis=1).astype(F32)
        far_norm, far_delta = stat_pair(far_tile)
        probs, dscores = block_terms(far_query, key, value, far_grad, far_norm, far_delta, None)
        add(1, dot(dscores, far_query) * SCALE)
        add(2, dot(probs, far_grad))


def plane_kernel(i_ref, r_ref, after_pair, o_ref):
    index = i_ref[0]
    row = index // 128
    layer = (index // 8) % DEPTH
    held = r_ref[...].astype(F32)
    query, key, value, grad = [
        held[:, tensor * 8 : (tensor + 1) * 8, :].reshape(128, WIDTH) for tensor in range(4)
    ]
    tile = jnp.sum(held[:, 32:FAR, :], axis=0)
    tile = jnp.concatenate([tile, jnp.zeros((8, 128), F32)], axis=0).astype(BF)
    depth = iota((128, WIDTH), 0) // RING
    for target in range(ROWS):
        cut = jnp.where(row < target, DEPTH, jnp.where(row == target, layer, 0))
        earlier = depth < cut
        o_ref[target, 0:128, :] = jnp.where(earlier, key, query).astype(BF)
        o_ref[target, 128:256, :] = jnp.where(earlier, value, grad).astype(BF)
        o_ref[target, 256:PLANE, :] = tile


def join_kernel(i_ref, f_ref, m_ref, n_ref, after, o_ref, sums, wide):
    index = i_ref[0]
    row = index // 128
    layer = (index // 8) % DEPTH
    place = index % RING
    here = row * DEPTH + layer
    sums[...] = n_ref[...]
    mine_all = m_ref[...].astype(F32)
    mine = [mine_all[tensor * 8 : (tensor + 1) * 8] for tensor in range(4)]
    stat_rows = [f_ref[y, 256:PLANE, :].astype(F32) for y in range(ROWS)]
    norm_row, delta_row = stat_pair(jnp.concatenate(stat_rows, axis=1))
    chosen = iota((8, 512), 1) == here * RING + iota((8, 512), 0)
    norm_column = jnp.sum(jnp.where(chosen, norm_row, 0.0), axis=1, keepdims=True)
    delta_column = jnp.sum(jnp.where(chosen, delta_row, 0.0), axis=1, keepdims=True)
    on_tail = iota((8, 128), 1) == 8 + iota((8, 128), 0)
    norm_tail = jnp.sum(jnp.where(on_tail, norm_column, 0.0), axis=0, keepdims=True)
    delta_tail = jnp.sum(jnp.where(on_tail, delta_column, 0.0), axis=0, keepdims=True)
    pad = jnp.zeros((112, WIDTH), F32)
    near_a = jnp.concatenate([mine[1], mine[0], pad], axis=0).astype(BF)
    near_b = jnp.concatenate([mine[2], mine[3], pad], axis=0).astype(BF)
    all_a = jnp.concatenate([f_ref[y, 0:128, :] for y in range(ROWS)] + [near_a], axis=0)
    all_b = jnp.concatenate([f_ref[y, 128:256, :] for y in range(ROWS)] + [near_b], axis=0)
    left = jnp.concatenate([mine[0], mine[1]], axis=0).astype(BF)
    right = jnp.concatenate([mine[3], mine[2]], axis=0).astype(BF)
    scores = dot_nt(left, all_a) * SCALE
    dprobs = dot_nt(right, all_b)
    norm_wide = jnp.concatenate([norm_row, norm_tail], axis=1)
    delta_wide = jnp.concatenate([delta_row, delta_tail], axis=1)
    norms = jnp.concatenate(
        [jnp.broadcast_to(norm_column, (8, 640)), jnp.broadcast_to(norm_wide, (8, 640))], axis=0
    )
    deltas = jnp.concatenate(
        [jnp.broadcast_to(delta_column, (8, 640)), jnp.broadcast_to(delta_wide, (8, 640))], axis=0
    )
    lane = iota((16, 640), 1)
    seat = iota((16, 640), 0)
    source = lane // RING
    tail = lane - 512
    low = jnp.where(lane < 512, source, jnp.where(tail < 8, here - 1 + (tail > seat), 1 << 20))
    high = jnp.where(
        lane < 512, source, jnp.where((tail >= 8) & (tail < 16), here + 1 - (tail < seat), -1)
    )
    valid = ((seat < 8) & (low < here)) | ((seat >= 8) & (high > here))
    probs = jnp.where(valid, jnp.exp(jnp.where(valid, scores - norms, 0.0)), 0.0)
    dscores = (probs * (dprobs - deltas)).astype(BF)
    wide[0:16, :] = dot(dscores, all_a) * SCALE
    wide[16:32, :] = dot(probs.astype(BF), all_b)
    for s in range(RING):
        for tensor, at in ((0, s), (1, 8 + s), (2, 24 + s)):
            span = pl.ds(tensor * SIDE + place // 4, 1)
            sums[s, span, :] = sums[s, span, :] + wide[at : at + 1, :]
    o_ref[...] = sums[...].astype(BF)


def post_kernel(r_ref, n_ref, q_ref, k_ref, v_ref):
    for tensor, ref in enumerate((q_ref, k_ref, v_ref)):
        for head in range(HEADS):
            residue = head % 4
            back = (iota((TOK, SIDE), 0) == 4 * iota((TOK, SIDE), 1) + residue).astype(BF)
            part = dot(back, r_ref[head, tensor * SIDE : (tensor + 1) * SIDE, :])
            ref[:, columns_of(head)] = (n_ref[tensor, :, columns_of(head)].astype(F32) + part).astype(BF)


def call(kernel, name, out, specs, scratch=(), flops=0, moved=0, places=None, limit=16):
    return pl.pallas_call(
        kernel,
        name=name,
        out_shape=out,
        in_specs=specs,
        out_specs=jax.tree.map(lambda _: VMEM, out) if places is None else places,
        scratch_shapes=list(scratch),
        cost_estimate=pl.CostEstimate(flops=flops, bytes_accessed=moved, transcendentals=0),
        compiler_params=pltpu.CompilerParams(vmem_limit_bytes=limit * 1024 * 1024),
    )


def shape(dims, dtype=BF):
    return jax.ShapeDtypeStruct(dims, dtype)


RING_GROUPS = [[base + i for i in range(RING)] for base in range(0, DEVICES, RING)]
DEPTH_GROUPS = [
    [y * 128 + z * 8 + i for z in range(DEPTH)] for y in range(ROWS) for i in range(RING)
]
ROW_GROUPS = [[y * 128 + i for y in range(ROWS)] for i in range(128)]


def exchange(array, groups):
    return lax.all_to_all(array, "seq", 0, 0, axis_index_groups=groups, tiled=True)


def partner(array, bit):
    return lax.ppermute(array, "seq", [(i, i ^ bit) for i in range(DEVICES)])


def body(query_rows, key_rows, value_rows, attn_out, out_grad, log_norms):
    index = lax.axis_index("seq").astype(jnp.int32).reshape(1)
    whole = (TOK, HEADS * WIDTH)
    side, stats = call(
        select_kernel,
        "select_rows",
        (shape((HEADS, CHUNK, WIDTH)), shape((16, HEADS * WIDTH))),
        [SMEM] + [ANY] * 6,
        [pltpu.VMEM(whole, BF)] * 5
        + [pltpu.VMEM((HEADS, TOK), F32), pltpu.SemaphoreType.DMA((6, 2))],
        flops=2 * 128 * 128 * 4096,
        moved=3 << 20,
        limit=60,
    )(index, query_rows, key_rows, value_rows, out_grad, attn_out, log_norms)
    side = exchange(side, RING_GROUPS)
    core, chip = call(
        payload_kernel,
        "near_payload",
        (shape((NEAR, HEADS * WIDTH)), shape((NEAR, HEADS * WIDTH))),
        [SMEM] + [ANY] * 5,
        [pltpu.SemaphoreType.DMA((2, 3))],
        moved=4 << 20,
        places=(ANY, ANY),
    )(index, query_rows, key_rows, value_rows, out_grad, stats)
    core, chip, relay = partner(core, 1), partner(chip, 2), partner(chip, 3)
    far, mine, pair = call(
        middle_kernel,
        "middle_rows",
        (shape((DEPTH, FAR, WIDTH)), shape((FAR, WIDTH)), shape((PAIR, WIDTH))),
        [SMEM, VMEM],
        [pltpu.VMEM((144, 128), F32)],
        moved=1 << 20,
    )(index, side)
    far = exchange(far, DEPTH_GROUPS)
    pair = partner(pair, 8)
    sums = call(
        pair_kernel,
        "pair_grads",
        shape((RING, OUT_CHUNK, WIDTH), F32),
        [SMEM, VMEM, VMEM, ANY],
        flops=20 * 2 * 10 * 128 * 256 * 256,
        moved=1 << 20,
    )(index, side, pair, chip)
    plane = call(
        plane_kernel,
        "plane_rows",
        shape((ROWS, PLANE, WIDTH)),
        [SMEM, VMEM, ANY],
        moved=1 << 20,
    )(index, far, sums)
    near_grads = call(
        near_kernel,
        "near_grads",
        shape((3, TOK, HEADS * WIDTH)),
        [SMEM] + [VMEM] * 8 + [ANY],
        flops=int(1 * 2 * 128 * 128 * 128 * 8 * 17),
        moved=4 << 20,
    )(index, query_rows, key_rows, value_rows, out_grad, stats, core, chip, relay, plane)
    plane = exchange(plane, ROW_GROUPS)
    grads = call(
        join_kernel,
        "join_grads",
        shape((RING, OUT_CHUNK, WIDTH)),
        [SMEM, VMEM, VMEM, VMEM, ANY],
        [pltpu.VMEM((RING, OUT_CHUNK, WIDTH), F32), pltpu.VMEM((128, 128), F32)],
        moved=1 << 20,
    )(index, plane, mine, sums, near_grads)
    grads = exchange(grads, RING_GROUPS)
    out = shape(whole)
    return call(
        post_kernel,
        "add_levels",
        (out, out, out),
        [VMEM] * 2,
        flops=2 * 128 * 32 * 3072,
        moved=4 << 20,
    )(grads, near_grads)


def solution(mesh):
    return jax.shard_map(
        body,
        mesh=mesh,
        in_specs=(
            P("seq", None),
            P("seq", None),
            P("seq", None),
            P("seq", None),
            P("seq", None),
            P(None, "seq"),
        ),
        out_specs=(P("seq", None), P("seq", None), P("seq", None)),
        check_vma=False,
    )
```

```python
import jax
import jax.numpy as jnp
from jax import lax
from jax.experimental import pallas as pl
from jax.experimental.pallas import tpu as pltpu
from jax.sharding import PartitionSpec as P

HEADS = 8
WIDTH = 128
TOK = 128
RING = 8
DEPTH = 16
ROWS = 4
DEVICES = 512
SCALE = WIDTH**-0.5
SIDE = 32
CHUNK = 4 * SIDE + 16
OUT_CHUNK = 3 * SIDE
PAIR = 4 * 128 + 32
FAR = 40
PLANE = 2 * 128 + 16
NEAR = 2 * TOK + 16

BF = jnp.bfloat16
F32 = jnp.float32
VMEM = pl.BlockSpec(memory_space=pltpu.VMEM)
SMEM = pl.BlockSpec(memory_space=pltpu.SMEM)
ANY = pl.BlockSpec(memory_space=pl.ANY)


def iota(shape, dim):
    return lax.broadcasted_iota(jnp.int32, shape, dim)


def dot(a, b):
    return jnp.dot(a, b, preferred_element_type=F32)


def dot_nt(a, b):
    return lax.dot_general(a, b, (((1,), (1,)), ((), ())), preferred_element_type=F32)


def dot_tn(a, b):
    return lax.dot_general(a, b, (((0,), (0,)), ((), ())), preferred_element_type=F32)


def split3(x):
    high = x.astype(BF).astype(F32)
    rest = x - high
    middle = rest.astype(BF).astype(F32)
    low = (rest - middle).astype(BF).astype(F32)
    return high, middle, low


def place3(parts, slot, first):
    high, middle, low = parts
    return jnp.where(
        slot == first,
        high,
        jnp.where(slot == first + 1, middle, jnp.where(slot == first + 2, low, 0.0)),
    )


def columns_of(head):
    return slice(head * WIDTH, (head + 1) * WIDTH)


def stat_pair(tile):
    norm = tile[0:1] + tile[1:2] + tile[2:3]
    delta = tile[3:4] + tile[4:5] + tile[5:6]
    return norm, delta


def block_terms(query, key, value, grad, norm, delta, mask):
    scores = dot_nt(key, query) * SCALE
    probs = jnp.exp(scores - norm)
    if mask is not None:
        probs = jnp.where(mask, probs, 0.0)
    dprobs = dot_nt(value, grad)
    dscores = (probs * (dprobs - delta)).astype(BF)
    return probs.astype(BF), dscores


def select_kernel(i_ref, q_in, k_in, v_in, g_in, o_in, n_in, out_ref, stat_ref, q, k, v, g, o, n, sems):
    copies = [[pltpu.make_async_copy(n_in, n, sems.at[0, 0])]]
    for number, (source, place) in enumerate(
        ((g_in, g), (o_in, o), (q_in, q), (k_in, k), (v_in, v))
    ):
        copies.append(
            [
                pltpu.make_async_copy(
                    source.at[pl.ds(part * TOK, TOK)],
                    place.at[pl.ds(part * TOK, TOK)],
                    sems.at[number + 1, part],
                )
                for part in range(1)
            ]
        )
    for group in copies:
        for copy in group:
            copy.start()
    seat = i_ref[0] % RING
    for group in copies[0:3]:
        for copy in group:
            copy.wait()
    lane = iota((TOK, 128), 1)
    spread = jnp.zeros((TOK, 128), F32)
    for head in range(HEADS):
        product = g[:, columns_of(head)].astype(F32) * o[:, columns_of(head)].astype(F32)
        total = jnp.sum(product, axis=-1, keepdims=True)
        spread = jnp.where(lane // 16 == head, total, spread)
    deltas = place3(split3(spread), lane % 16, 3)
    norms = jnp.broadcast_to(n[...][:, None, :], (HEADS, 16, TOK)).reshape(128, TOK)
    norms = place3(split3(norms), iota((128, TOK), 0) % 16, 0)
    stats = (norms + deltas.T).astype(BF)
    for head in range(HEADS):
        stat_ref[:, columns_of(head)] = stats[head * 16 : (head + 1) * 16, :]
    token = iota((TOK, 128), 0)
    for residue in range(4):
        spot = ((token == 4 * (lane % SIDE) + residue) & (lane // SIDE == seat % 4)).astype(BF)
        placed = dot(stats, spot).astype(BF)
        for head in (residue, residue + 4):
            out_ref[head, 4 * SIDE : CHUNK, :] = placed[head * 16 : (head + 1) * 16, :]
    order = iota((TOK, TOK), 0)
    perm = (4 * (order % SIDE) + order // SIDE == iota((TOK, TOK), 1)).astype(BF)
    for tensor, (ref, group) in enumerate(
        ((q, copies[3]), (k, copies[4]), (v, copies[5]), (g, ()))
    ):
        for copy in group:
            copy.wait()
        ordered = dot(perm, ref[...]).astype(BF)
        for head in range(HEADS):
            start = SIDE * (head % 4)
            out_ref[head, tensor * SIDE : (tensor + 1) * SIDE, :] = ordered[
                start : start + SIDE, columns_of(head)
            ]


def payload_kernel(i_ref, q_in, k_in, v_in, g_in, s_in, core_ref, chip_ref, sems):
    index = i_ref[0]
    for number, (ref, bit) in enumerate(((core_ref, 1), (chip_ref, 2))):
        later = (index & bit) != 0

        def send(first, second, ref=ref, number=number):
            copies = [
                pltpu.make_async_copy(first, ref.at[pl.ds(0, TOK)], sems.at[number, 0]),
                pltpu.make_async_copy(second, ref.at[pl.ds(TOK, TOK)], sems.at[number, 1]),
                pltpu.make_async_copy(s_in, ref.at[pl.ds(2 * TOK, 16)], sems.at[number, 2]),
            ]
            for copy in copies:
                copy.start()
            for copy in copies:
                copy.wait()

        @pl.when(later)
        def _():
            send(q_in, g_in)

        @pl.when(jnp.logical_not(later))
        def _():
            send(k_in, v_in)


def near_kernel(i_ref, q, k, v, g, s, r1, r2, r3, after, out_ref):
    place = i_ref[0] % 4
    stat_rows = [stat_pair(s[:, columns_of(head)].astype(F32)) for head in range(HEADS)]
    stat_rows = [row[0] for row in stat_rows] + [row[1] for row in stat_rows]
    stat_columns = jnp.concatenate(stat_rows + [jnp.zeros((112, TOK), F32)], axis=0).T
    blocks = (r1, r2, r3)
    causal = iota((TOK, TOK), 1) <= iota((TOK, TOK), 0)

    def part(block, number, c):
        return block[number * TOK : (TOK, 2 * TOK, NEAR)[number], c]

    def terms(earlier, later):
        for head in range(HEADS):
            c = columns_of(head)
            query, grad = q[:, c], g[:, c]
            key = jnp.concatenate([k[:, c]] + [part(block, 0, c) for block in earlier], axis=0)
            value = jnp.concatenate([v[:, c]] + [part(block, 1, c) for block in earlier], axis=0)
            size = key.shape[0]
            norm = stat_columns[:, head : head + 1]
            delta = stat_columns[:, HEADS + head : HEADS + head + 1]
            probs = jnp.exp(dot_nt(query, key) * SCALE - norm)
            own = jnp.where(causal, probs[:, 0:TOK], 0.0)
            probs = own if size == TOK else jnp.concatenate([own, probs[:, TOK:]], axis=1)
            dscores = (probs * (dot_nt(grad, value) - delta)).astype(BF)
            out_ref[0, :, c] = (dot(dscores, key) * SCALE).astype(BF)
            key_grad = dot_tn(dscores[:, 0:TOK], query)
            value_grad = dot_tn(own.astype(BF), grad)
            if later:
                query = jnp.concatenate([part(block, 0, c) for block in later], axis=0)
                grad = jnp.concatenate([part(block, 1, c) for block in later], axis=0)
                tile = jnp.concatenate([part(block, 2, c) for block in later], axis=1)
                norm, delta = stat_pair(tile.astype(F32))
                probs, dscores = block_terms(query, k[:, c], v[:, c], grad, norm, delta, None)
                key_grad = key_grad + dot(dscores, query)
                value_grad = value_grad + dot(probs, grad)
            out_ref[1, :, c] = (key_grad * SCALE).astype(BF)
            out_ref[2, :, c] = value_grad.astype(BF)

    cases = (
        ((), (0, 1, 2)),
        ((0,), (1, 2)),
        ((1, 2), (0,)),
        ((0, 1, 2), ()),
    )
    for number, (earlier, later) in enumerate(cases):

        @pl.when(place == number)
        def _(earlier=earlier, later=later):
            terms([blocks[i] for i in earlier], [blocks[i] for i in later])


def middle_kernel(i_ref, r_ref, far_ref, mine_ref, pair_ref, flat):
    index = i_ref[0]
    layer = (index // 8) % DEPTH
    place = index % RING
    upper = layer % 2 == 1
    lane = iota((16, 128), 1)
    tiles = [r_ref[s, 4 * SIDE : CHUNK, :].astype(F32) for s in range(RING)]
    stats = jnp.zeros((16, 128), F32)
    for s in range(RING):
        taken = jnp.where(lane == (s % 4) * SIDE + place // 4, tiles[s], 0.0)
        value = jnp.sum(taken, axis=1, keepdims=True)
        stats = jnp.where(lane == layer * RING + s, value, stats)
    rows = []
    for tensor in range(4):
        first = tensor * SIDE
        flat[0:128] = r_ref[:, first : first + 16, :].astype(F32).reshape(128, WIDTH)
        rows.append(flat[pl.ds(place // 4, RING, stride=16), :])
    payload = jnp.concatenate(rows + [stats[0:8]], axis=0).astype(BF)
    mine_ref[...] = payload
    for target in range(DEPTH):
        far_ref[target] = payload

    def fill(first, second):
        for number, tensor in enumerate((first, second)):
            pair_ref[number * 256 : (number + 1) * 256, :] = r_ref[
                :, tensor * SIDE : (tensor + 1) * SIDE, :
            ].reshape(256, WIDTH)

    @pl.when(upper)
    def _():
        fill(0, 3)

    @pl.when(jnp.logical_not(upper))
    def _():
        fill(1, 2)

    pair_ref[512:528, :] = (tiles[0] + tiles[1] + tiles[2] + tiles[3]).astype(BF)
    pair_ref[528:544, :] = (tiles[4] + tiles[5] + tiles[6] + tiles[7]).astype(BF)


def pair_kernel(i_ref, r_ref, x_ref, after, o_ref):
    upper = (i_ref[0] // 8) % 2 == 1

    def own(tensor):
        return r_ref[:, tensor * SIDE : (tensor + 1) * SIDE, :].reshape(256, WIDTH)

    def put(tensor, part):
        o_ref[:, tensor * SIDE : (tensor + 1) * SIDE, :] = part.reshape(RING, SIDE, WIDTH)

    def add(tensor, part):
        span = slice(tensor * SIDE, (tensor + 1) * SIDE)
        o_ref[:, span, :] = o_ref[:, span, :] + part.reshape(RING, SIDE, WIDTH)

    tiles = [r_ref[s, 4 * SIDE : CHUNK, :].astype(F32) for s in range(RING)]
    own_tile = jnp.concatenate(
        [tiles[0] + tiles[1] + tiles[2] + tiles[3], tiles[4] + tiles[5] + tiles[6] + tiles[7]],
        axis=1,
    )
    norm, delta = stat_pair(own_tile)
    query, key, value, grad = own(0), own(1), own(2), own(3)
    causal = iota((256, 256), 0) <= iota((256, 256), 1)
    probs, dscores = block_terms(query, key, value, grad, norm, delta, causal)
    put(0, dot_tn(dscores, key) * SCALE)
    put(1, dot(dscores, query) * SCALE)
    put(2, dot(probs, grad))

    @pl.when(upper)
    def _():
        far_key = x_ref[0:256, :]
        far_value = x_ref[256:512, :]
        _, dscores = block_terms(query, far_key, far_value, grad, norm, delta, None)
        add(0, dot_tn(dscores, far_key) * SCALE)

    @pl.when(jnp.logical_not(upper))
    def _():
        far_query = x_ref[0:256, :]
        far_grad = x_ref[256:512, :]
        far_tile = jnp.concatenate([x_ref[512:528, :], x_ref[528:544, :]], axis=1).astype(F32)
        far_norm, far_delta = stat_pair(far_tile)
        probs, dscores = block_terms(far_query, key, value, far_grad, far_norm, far_delta, None)
        add(1, dot(dscores, far_query) * SCALE)
        add(2, dot(probs, far_grad))


def plane_kernel(i_ref, r_ref, after_pair, o_ref):
    index = i_ref[0]
    row = index // 128
    layer = (index // 8) % DEPTH
    held = r_ref[...].astype(F32)
    query, key, value, grad = [
        held[:, tensor * 8 : (tensor + 1) * 8, :].reshape(128, WIDTH) for tensor in range(4)
    ]
    tile = jnp.sum(held[:, 32:FAR, :], axis=0)
    tile = jnp.concatenate([tile, jnp.zeros((8, 128), F32)], axis=0).astype(BF)
    depth = iota((128, WIDTH), 0) // RING
    for target in range(ROWS):
        cut = jnp.where(row < target, DEPTH, jnp.where(row == target, layer, 0))
        earlier = depth < cut
        o_ref[target, 0:128, :] = jnp.where(earlier, key, query).astype(BF)
        o_ref[target, 128:256, :] = jnp.where(earlier, value, grad).astype(BF)
        o_ref[target, 256:PLANE, :] = tile


def join_kernel(i_ref, f_ref, m_ref, n_ref, after, o_ref, sums, wide):
    index = i_ref[0]
    row = index // 128
    layer = (index // 8) % DEPTH
    place = index % RING
    here = row * DEPTH + layer
    sums[...] = n_ref[...]
    mine_all = m_ref[...].astype(F32)
    mine = [mine_all[tensor * 8 : (tensor + 1) * 8] for tensor in range(4)]
    stat_rows = [f_ref[y, 256:PLANE, :].astype(F32) for y in range(ROWS)]
    norm_row, delta_row = stat_pair(jnp.concatenate(stat_rows, axis=1))
    chosen = iota((8, 512), 1) == here * RING + iota((8, 512), 0)
    norm_column = jnp.sum(jnp.where(chosen, norm_row, 0.0), axis=1, keepdims=True)
    delta_column = jnp.sum(jnp.where(chosen, delta_row, 0.0), axis=1, keepdims=True)
    on_tail = iota((8, 128), 1) == 8 + iota((8, 128), 0)
    norm_tail = jnp.sum(jnp.where(on_tail, norm_column, 0.0), axis=0, keepdims=True)
    delta_tail = jnp.sum(jnp.where(on_tail, delta_column, 0.0), axis=0, keepdims=True)
    pad = jnp.zeros((112, WIDTH), F32)
    near_a = jnp.concatenate([mine[1], mine[0], pad], axis=0).astype(BF)
    near_b = jnp.concatenate([mine[2], mine[3], pad], axis=0).astype(BF)
    all_a = jnp.concatenate([f_ref[y, 0:128, :] for y in range(ROWS)] + [near_a], axis=0)
    all_b = jnp.concatenate([f_ref[y, 128:256, :] for y in range(ROWS)] + [near_b], axis=0)
    left = jnp.concatenate([mine[0], mine[1]], axis=0).astype(BF)
    right = jnp.concatenate([mine[3], mine[2]], axis=0).astype(BF)
    scores = dot_nt(left, all_a) * SCALE
    dprobs = dot_nt(right, all_b)
    norm_wide = jnp.concatenate([norm_row, norm_tail], axis=1)
    delta_wide = jnp.concatenate([delta_row, delta_tail], axis=1)
    norms = jnp.concatenate(
        [jnp.broadcast_to(norm_column, (8, 640)), jnp.broadcast_to(norm_wide, (8, 640))], axis=0
    )
    deltas = jnp.concatenate(
        [jnp.broadcast_to(delta_column, (8, 640)), jnp.broadcast_to(delta_wide, (8, 640))], axis=0
    )
    lane = iota((16, 640), 1)
    seat = iota((16, 640), 0)
    source = lane // RING
    tail = lane - 512
    low = jnp.where(lane < 512, source, jnp.where(tail < 8, here - 1 + (tail > seat), 1 << 20))
    high = jnp.where(
        lane < 512, source, jnp.where((tail >= 8) & (tail < 16), here + 1 - (tail < seat), -1)
    )
    valid = ((seat < 8) & (low < here)) | ((seat >= 8) & (high > here))
    probs = jnp.where(valid, jnp.exp(jnp.where(valid, scores - norms, 0.0)), 0.0)
    dscores = (probs * (dprobs - deltas)).astype(BF)
    wide[0:16, :] = dot(dscores, all_a) * SCALE
    wide[16:32, :] = dot(probs.astype(BF), all_b)
    for s in range(RING):
        for tensor, at in ((0, s), (1, 8 + s), (2, 24 + s)):
            span = pl.ds(tensor * SIDE + place // 4, 1)
            sums[s, span, :] = sums[s, span, :] + wide[at : at + 1, :]
    o_ref[...] = sums[...].astype(BF)


def post_kernel(r_ref, n_ref, q_ref, k_ref, v_ref):
    for tensor, ref in enumerate((q_ref, k_ref, v_ref)):
        for head in range(HEADS):
            residue = head % 4
            back = (iota((TOK, SIDE), 0) == 4 * iota((TOK, SIDE), 1) + residue).astype(BF)
            part = dot(back, r_ref[head, tensor * SIDE : (tensor + 1) * SIDE, :])
            ref[:, columns_of(head)] = (n_ref[tensor, :, columns_of(head)].astype(F32) + part).astype(BF)


def call(kernel, name, out, specs, scratch=(), flops=0, moved=0, places=None, limit=16):
    return pl.pallas_call(
        kernel,
        name=name,
        out_shape=out,
        in_specs=specs,
        out_specs=jax.tree.map(lambda _: VMEM, out) if places is None else places,
        scratch_shapes=list(scratch),
        cost_estimate=pl.CostEstimate(flops=flops, bytes_accessed=moved, transcendentals=0),
        compiler_params=pltpu.CompilerParams(vmem_limit_bytes=limit * 1024 * 1024),
    )


def shape(dims, dtype=BF):
    return jax.ShapeDtypeStruct(dims, dtype)


RING_GROUPS = [[base + i for i in range(RING)] for base in range(0, DEVICES, RING)]
DEPTH_GROUPS = [
    [y * 128 + z * 8 + i for z in range(DEPTH)] for y in range(ROWS) for i in range(RING)
]
ROW_GROUPS = [[y * 128 + i for y in range(ROWS)] for i in range(128)]


def exchange(array, groups):
    return lax.all_to_all(array, "seq", 0, 0, axis_index_groups=groups, tiled=True)


def partner(array, bit):
    return lax.ppermute(array, "seq", [(i, i ^ bit) for i in range(DEVICES)])


def body(query_rows, key_rows, value_rows, attn_out, out_grad, log_norms):
    index = lax.axis_index("seq").astype(jnp.int32).reshape(1)
    whole = (TOK, HEADS * WIDTH)
    side, stats = call(
        select_kernel,
        "select_rows",
        (shape((HEADS, CHUNK, WIDTH)), shape((16, HEADS * WIDTH))),
        [SMEM] + [ANY] * 6,
        [pltpu.VMEM(whole, BF)] * 5
        + [pltpu.VMEM((HEADS, TOK), F32), pltpu.SemaphoreType.DMA((6, 2))],
        flops=2 * 128 * 128 * 4096,
        moved=3 << 20,
        limit=60,
    )(index, query_rows, key_rows, value_rows, out_grad, attn_out, log_norms)
    side = exchange(side, RING_GROUPS)
    core, chip = call(
        payload_kernel,
        "near_payload",
        (shape((NEAR, HEADS * WIDTH)), shape((NEAR, HEADS * WIDTH))),
        [SMEM] + [ANY] * 5,
        [pltpu.SemaphoreType.DMA((2, 3))],
        moved=4 << 20,
        places=(ANY, ANY),
    )(index, query_rows, key_rows, value_rows, out_grad, stats)
    core, chip, relay = partner(core, 1), partner(chip, 2), partner(chip, 3)
    far, mine, pair = call(
        middle_kernel,
        "middle_rows",
        (shape((DEPTH, FAR, WIDTH)), shape((FAR, WIDTH)), shape((PAIR, WIDTH))),
        [SMEM, VMEM],
        [pltpu.VMEM((144, 128), F32)],
        moved=1 << 20,
    )(index, side)
    far = exchange(far, DEPTH_GROUPS)
    pair = partner(pair, 8)
    sums = call(
        pair_kernel,
        "pair_grads",
        shape((RING, OUT_CHUNK, WIDTH), F32),
        [SMEM, VMEM, VMEM, ANY],
        flops=20 * 2 * 10 * 128 * 256 * 256,
        moved=1 << 20,
    )(index, side, pair, chip)
    plane = call(
        plane_kernel,
        "plane_rows",
        shape((ROWS, PLANE, WIDTH)),
        [SMEM, VMEM, ANY],
        moved=1 << 20,
    )(index, far, sums)
    near_grads = call(
        near_kernel,
        "near_grads",
        shape((3, TOK, HEADS * WIDTH)),
        [SMEM] + [VMEM] * 8 + [ANY],
        flops=int(1 * 2 * 128 * 128 * 128 * 8 * 17),
        moved=4 << 20,
    )(index, query_rows, key_rows, value_rows, out_grad, stats, core, chip, relay, plane)
    plane = exchange(plane, ROW_GROUPS)
    grads = call(
        join_kernel,
        "join_grads",
        shape((RING, OUT_CHUNK, WIDTH)),
        [SMEM, VMEM, VMEM, VMEM, ANY],
        [pltpu.VMEM((RING, OUT_CHUNK, WIDTH), F32), pltpu.VMEM((128, 128), F32)],
        moved=1 << 20,
    )(index, plane, mine, sums, near_grads)
    grads = exchange(grads, RING_GROUPS)
    out = shape(whole)
    return call(
        post_kernel,
        "add_levels",
        (out, out, out),
        [VMEM] * 2,
        flops=2 * 128 * 32 * 3072,
        moved=4 << 20,
    )(grads, near_grads)


def solution(mesh):
    return jax.shard_map(
        body,
        mesh=mesh,
        in_specs=(
            P("seq", None),
            P("seq", None),
            P("seq", None),
            P("seq", None),
            P("seq", None),
            P(None, "seq"),
        ),
        out_specs=(P("seq", None), P("seq", None), P("seq", None)),
        check_vma=False,
    )
```

```python
import jax
import jax.numpy as jnp
from jax import lax
from jax.experimental import pallas as pl
from jax.experimental.pallas import tpu as pltpu
from jax.sharding import PartitionSpec as P

HEADS = 8
WIDTH = 128
TOK = 128
RING = 8
DEPTH = 16
ROWS = 4
DEVICES = 512
SCALE = WIDTH**-0.5
SIDE = 32
CHUNK = 4 * SIDE + 16
OUT_CHUNK = 3 * SIDE
PAIR = 4 * 128 + 32
FAR = 40
PLANE = 2 * 128 + 16
NEAR = 2 * TOK + 16

BF = jnp.bfloat16
F32 = jnp.float32
VMEM = pl.BlockSpec(memory_space=pltpu.VMEM)
SMEM = pl.BlockSpec(memory_space=pltpu.SMEM)
ANY = pl.BlockSpec(memory_space=pl.ANY)


def iota(shape, dim):
    return lax.broadcasted_iota(jnp.int32, shape, dim)


def dot(a, b):
    return jnp.dot(a, b, preferred_element_type=F32)


def dot_nt(a, b):
    return lax.dot_general(a, b, (((1,), (1,)), ((), ())), preferred_element_type=F32)


def dot_tn(a, b):
    return lax.dot_general(a, b, (((0,), (0,)), ((), ())), preferred_element_type=F32)


def split3(x):
    high = x.astype(BF).astype(F32)
    rest = x - high
    middle = rest.astype(BF).astype(F32)
    low = (rest - middle).astype(BF).astype(F32)
    return high, middle, low


def place3(parts, slot, first):
    high, middle, low = parts
    return jnp.where(
        slot == first,
        high,
        jnp.where(slot == first + 1, middle, jnp.where(slot == first + 2, low, 0.0)),
    )


def columns_of(head):
    return slice(head * WIDTH, (head + 1) * WIDTH)


def stat_pair(tile):
    norm = tile[0:1] + tile[1:2] + tile[2:3]
    delta = tile[3:4] + tile[4:5] + tile[5:6]
    return norm, delta


def block_terms(query, key, value, grad, norm, delta, mask):
    scores = dot_nt(key, query) * SCALE
    probs = jnp.exp(scores - norm)
    if mask is not None:
        probs = jnp.where(mask, probs, 0.0)
    dprobs = dot_nt(value, grad)
    dscores = (probs * (dprobs - delta)).astype(BF)
    return probs.astype(BF), dscores


def select_kernel(i_ref, q_in, k_in, v_in, g_in, o_in, n_in, out_ref, stat_ref, q, k, v, g, o, n, sems):
    copies = [[pltpu.make_async_copy(n_in, n, sems.at[0, 0])]]
    for number, (source, place) in enumerate(
        ((g_in, g), (o_in, o), (q_in, q), (k_in, k), (v_in, v))
    ):
        copies.append(
            [
                pltpu.make_async_copy(
                    source.at[pl.ds(part * 64, 64)],
                    place.at[pl.ds(part * 64, 64)],
                    sems.at[number + 1, part],
                )
                for part in range(2)
            ]
        )
    for group in copies:
        for copy in group:
            copy.start()
    seat = i_ref[0] % RING
    for group in copies[0:3]:
        for copy in group:
            copy.wait()
    lane = iota((TOK, 128), 1)
    spread = jnp.zeros((TOK, 128), F32)
    for head in range(HEADS):
        product = g[:, columns_of(head)].astype(F32) * o[:, columns_of(head)].astype(F32)
        total = jnp.sum(product, axis=-1, keepdims=True)
        spread = jnp.where(lane // 16 == head, total, spread)
    deltas = place3(split3(spread), lane % 16, 3)
    norms = jnp.broadcast_to(n[...][:, None, :], (HEADS, 16, TOK)).reshape(128, TOK)
    norms = place3(split3(norms), iota((128, TOK), 0) % 16, 0)
    stats = (norms + deltas.T).astype(BF)
    for head in range(HEADS):
        stat_ref[:, columns_of(head)] = stats[head * 16 : (head + 1) * 16, :]
    token = iota((TOK, 128), 0)
    for residue in range(4):
        spot = ((token == 4 * (lane % SIDE) + residue) & (lane // SIDE == seat % 4)).astype(BF)
        placed = dot(stats, spot).astype(BF)
        for head in (residue, residue + 4):
            out_ref[head, 4 * SIDE : CHUNK, :] = placed[head * 16 : (head + 1) * 16, :]
    order = iota((TOK, TOK), 0)
    perm = (4 * (order % SIDE) + order // SIDE == iota((TOK, TOK), 1)).astype(BF)
    for tensor, (ref, group) in enumerate(
        ((q, copies[3]), (k, copies[4]), (v, copies[5]), (g, ()))
    ):
        for copy in group:
            copy.wait()
        ordered = dot(perm, ref[...]).astype(BF)
        for head in range(HEADS):
            start = SIDE * (head % 4)
            out_ref[head, tensor * SIDE : (tensor + 1) * SIDE, :] = ordered[
                start : start + SIDE, columns_of(head)
            ]


def payload_kernel(i_ref, q_in, k_in, v_in, g_in, s_in, core_ref, chip_ref, sems):
    index = i_ref[0]
    for number, (ref, bit) in enumerate(((core_ref, 1), (chip_ref, 2))):
        later = (index & bit) != 0

        def send(first, second, ref=ref, number=number):
            copies = [
                pltpu.make_async_copy(first, ref.at[pl.ds(0, TOK)], sems.at[number, 0]),
                pltpu.make_async_copy(second, ref.at[pl.ds(TOK, TOK)], sems.at[number, 1]),
                pltpu.make_async_copy(s_in, ref.at[pl.ds(2 * TOK, 16)], sems.at[number, 2]),
            ]
            for copy in copies:
                copy.start()
            for copy in copies:
                copy.wait()

        @pl.when(later)
        def _():
            send(q_in, g_in)

        @pl.when(jnp.logical_not(later))
        def _():
            send(k_in, v_in)


def near_kernel(i_ref, q, k, v, g, s, r1, r2, r3, after, out_ref):
    place = i_ref[0] % 4
    stat_rows = [stat_pair(s[:, columns_of(head)].astype(F32)) for head in range(HEADS)]
    stat_rows = [row[0] for row in stat_rows] + [row[1] for row in stat_rows]
    stat_columns = jnp.concatenate(stat_rows + [jnp.zeros((112, TOK), F32)], axis=0).T
    blocks = (r1, r2, r3)

    def part(block, number, c):
        return block[number * TOK : (TOK, 2 * TOK, NEAR)[number], c]

    def terms(earlier, later):
        for head in range(HEADS):
            c = columns_of(head)
            query, grad = q[:, c], g[:, c]
            key = jnp.concatenate([k[:, c]] + [part(block, 0, c) for block in earlier], axis=0)
            value = jnp.concatenate([v[:, c]] + [part(block, 1, c) for block in earlier], axis=0)
            size = key.shape[0]
            norm = stat_columns[:, head : head + 1]
            delta = stat_columns[:, HEADS + head : HEADS + head + 1]
            lane = iota((TOK, size), 1)
            mask = (lane <= iota((TOK, size), 0)) | (lane >= TOK)
            probs = jnp.where(mask, jnp.exp(dot_nt(query, key) * SCALE - norm), 0.0)
            dscores = (probs * (dot_nt(grad, value) - delta)).astype(BF)
            out_ref[0, :, c] = (dot(dscores, key) * SCALE).astype(BF)
            key_grad = dot_tn(dscores[:, 0:TOK], query)
            value_grad = dot_tn(probs[:, 0:TOK].astype(BF), grad)
            if later:
                query = jnp.concatenate([part(block, 0, c) for block in later], axis=0)
                grad = jnp.concatenate([part(block, 1, c) for block in later], axis=0)
                tile = jnp.concatenate([part(block, 2, c) for block in later], axis=1)
                norm, delta = stat_pair(tile.astype(F32))
                probs, dscores = block_terms(query, k[:, c], v[:, c], grad, norm, delta, None)
                key_grad = key_grad + dot(dscores, query)
                value_grad = value_grad + dot(probs, grad)
            out_ref[1, :, c] = (key_grad * SCALE).astype(BF)
            out_ref[2, :, c] = value_grad.astype(BF)

    cases = (
        ((), (0, 1, 2)),
        ((0,), (1, 2)),
        ((1, 2), (0,)),
        ((0, 1, 2), ()),
    )
    for number, (earlier, later) in enumerate(cases):

        @pl.when(place == number)
        def _(earlier=earlier, later=later):
            terms([blocks[i] for i in earlier], [blocks[i] for i in later])


def middle_kernel(i_ref, r_ref, far_ref, mine_ref, pair_ref, flat):
    index = i_ref[0]
    layer = (index // 8) % DEPTH
    place = index % RING
    upper = layer % 2 == 1
    lane = iota((16, 128), 1)
    tiles = [r_ref[s, 4 * SIDE : CHUNK, :].astype(F32) for s in range(RING)]
    stats = jnp.zeros((16, 128), F32)
    for s in range(RING):
        taken = jnp.where(lane == (s % 4) * SIDE + place // 4, tiles[s], 0.0)
        value = jnp.sum(taken, axis=1, keepdims=True)
        stats = jnp.where(lane == layer * RING + s, value, stats)
    rows = []
    for tensor in range(4):
        first = tensor * SIDE
        flat[0:128] = r_ref[:, first : first + 16, :].astype(F32).reshape(128, WIDTH)
        rows.append(flat[pl.ds(place // 4, RING, stride=16), :])
    payload = jnp.concatenate(rows + [stats[0:8]], axis=0).astype(BF)
    mine_ref[...] = payload
    for target in range(DEPTH):
        far_ref[target] = payload

    def fill(first, second):
        for number, tensor in enumerate((first, second)):
            pair_ref[number * 256 : (number + 1) * 256, :] = r_ref[
                :, tensor * SIDE : (tensor + 1) * SIDE, :
            ].reshape(256, WIDTH)

    @pl.when(upper)
    def _():
        fill(0, 3)

    @pl.when(jnp.logical_not(upper))
    def _():
        fill(1, 2)

    pair_ref[512:528, :] = (tiles[0] + tiles[1] + tiles[2] + tiles[3]).astype(BF)
    pair_ref[528:544, :] = (tiles[4] + tiles[5] + tiles[6] + tiles[7]).astype(BF)


def pair_kernel(i_ref, r_ref, x_ref, after, o_ref):
    upper = (i_ref[0] // 8) % 2 == 1

    def own(tensor):
        return r_ref[:, tensor * SIDE : (tensor + 1) * SIDE, :].reshape(256, WIDTH)

    def put(tensor, part):
        o_ref[:, tensor * SIDE : (tensor + 1) * SIDE, :] = part.reshape(RING, SIDE, WIDTH)

    def add(tensor, part):
        span = slice(tensor * SIDE, (tensor + 1) * SIDE)
        o_ref[:, span, :] = o_ref[:, span, :] + part.reshape(RING, SIDE, WIDTH)

    tiles = [r_ref[s, 4 * SIDE : CHUNK, :].astype(F32) for s in range(RING)]
    own_tile = jnp.concatenate(
        [tiles[0] + tiles[1] + tiles[2] + tiles[3], tiles[4] + tiles[5] + tiles[6] + tiles[7]],
        axis=1,
    )
    norm, delta = stat_pair(own_tile)
    query, key, value, grad = own(0), own(1), own(2), own(3)
    causal = iota((256, 256), 0) <= iota((256, 256), 1)
    probs, dscores = block_terms(query, key, value, grad, norm, delta, causal)
    put(0, dot_tn(dscores, key) * SCALE)
    put(1, dot(dscores, query) * SCALE)
    put(2, dot(probs, grad))

    @pl.when(upper)
    def _():
        far_key = x_ref[0:256, :]
        far_value = x_ref[256:512, :]
        _, dscores = block_terms(query, far_key, far_value, grad, norm, delta, None)
        add(0, dot_tn(dscores, far_key) * SCALE)

    @pl.when(jnp.logical_not(upper))
    def _():
        far_query = x_ref[0:256, :]
        far_grad = x_ref[256:512, :]
        far_tile = jnp.concatenate([x_ref[512:528, :], x_ref[528:544, :]], axis=1).astype(F32)
        far_norm, far_delta = stat_pair(far_tile)
        probs, dscores = block_terms(far_query, key, value, far_grad, far_norm, far_delta, None)
        add(1, dot(dscores, far_query) * SCALE)
        add(2, dot(probs, far_grad))


def plane_kernel(i_ref, r_ref, after_pair, o_ref):
    index = i_ref[0]
    row = index // 128
    layer = (index // 8) % DEPTH
    held = r_ref[...].astype(F32)
    query, key, value, grad = [
        held[:, tensor * 8 : (tensor + 1) * 8, :].reshape(128, WIDTH) for tensor in range(4)
    ]
    tile = jnp.sum(held[:, 32:FAR, :], axis=0)
    tile = jnp.concatenate([tile, jnp.zeros((8, 128), F32)], axis=0).astype(BF)
    depth = iota((128, WIDTH), 0) // RING
    for target in range(ROWS):
        cut = jnp.where(row < target, DEPTH, jnp.where(row == target, layer, 0))
        earlier = depth < cut
        o_ref[target, 0:128, :] = jnp.where(earlier, key, query).astype(BF)
        o_ref[target, 128:256, :] = jnp.where(earlier, value, grad).astype(BF)
        o_ref[target, 256:PLANE, :] = tile


def join_kernel(i_ref, f_ref, m_ref, n_ref, after, o_ref, sums, wide):
    index = i_ref[0]
    row = index // 128
    layer = (index // 8) % DEPTH
    place = index % RING
    here = row * DEPTH + layer
    sums[...] = n_ref[...]
    mine_all = m_ref[...].astype(F32)
    mine = [mine_all[tensor * 8 : (tensor + 1) * 8] for tensor in range(4)]
    stat_rows = [f_ref[y, 256:PLANE, :].astype(F32) for y in range(ROWS)]
    norm_row, delta_row = stat_pair(jnp.concatenate(stat_rows, axis=1))
    chosen = iota((8, 512), 1) == here * RING + iota((8, 512), 0)
    norm_column = jnp.sum(jnp.where(chosen, norm_row, 0.0), axis=1, keepdims=True)
    delta_column = jnp.sum(jnp.where(chosen, delta_row, 0.0), axis=1, keepdims=True)
    on_tail = iota((8, 128), 1) == 8 + iota((8, 128), 0)
    norm_tail = jnp.sum(jnp.where(on_tail, norm_column, 0.0), axis=0, keepdims=True)
    delta_tail = jnp.sum(jnp.where(on_tail, delta_column, 0.0), axis=0, keepdims=True)
    pad = jnp.zeros((112, WIDTH), F32)
    near_a = jnp.concatenate([mine[1], mine[0], pad], axis=0).astype(BF)
    near_b = jnp.concatenate([mine[2], mine[3], pad], axis=0).astype(BF)
    all_a = jnp.concatenate([f_ref[y, 0:128, :] for y in range(ROWS)] + [near_a], axis=0)
    all_b = jnp.concatenate([f_ref[y, 128:256, :] for y in range(ROWS)] + [near_b], axis=0)
    left = jnp.concatenate([mine[0], mine[1]], axis=0).astype(BF)
    right = jnp.concatenate([mine[3], mine[2]], axis=0).astype(BF)
    scores = dot_nt(left, all_a) * SCALE
    dprobs = dot_nt(right, all_b)
    norm_wide = jnp.concatenate([norm_row, norm_tail], axis=1)
    delta_wide = jnp.concatenate([delta_row, delta_tail], axis=1)
    norms = jnp.concatenate(
        [jnp.broadcast_to(norm_column, (8, 640)), jnp.broadcast_to(norm_wide, (8, 640))], axis=0
    )
    deltas = jnp.concatenate(
        [jnp.broadcast_to(delta_column, (8, 640)), jnp.broadcast_to(delta_wide, (8, 640))], axis=0
    )
    lane = iota((16, 640), 1)
    seat = iota((16, 640), 0)
    source = lane // RING
    tail = lane - 512
    low = jnp.where(lane < 512, source, jnp.where(tail < 8, here - 1 + (tail > seat), 1 << 20))
    high = jnp.where(
        lane < 512, source, jnp.where((tail >= 8) & (tail < 16), here + 1 - (tail < seat), -1)
    )
    valid = ((seat < 8) & (low < here)) | ((seat >= 8) & (high > here))
    probs = jnp.where(valid, jnp.exp(jnp.where(valid, scores - norms, 0.0)), 0.0)
    dscores = (probs * (dprobs - deltas)).astype(BF)
    wide[0:16, :] = dot(dscores, all_a) * SCALE
    wide[16:32, :] = dot(probs.astype(BF), all_b)
    for s in range(RING):
        for tensor, at in ((0, s), (1, 8 + s), (2, 24 + s)):
            span = pl.ds(tensor * SIDE + place // 4, 1)
            sums[s, span, :] = sums[s, span, :] + wide[at : at + 1, :]
    o_ref[...] = sums[...].astype(BF)


def post_kernel(r_ref, n_ref, q_ref, k_ref, v_ref):
    for tensor, ref in enumerate((q_ref, k_ref, v_ref)):
        for head in range(HEADS):
            residue = head % 4
            back = (iota((TOK, SIDE), 0) == 4 * iota((TOK, SIDE), 1) + residue).astype(BF)
            part = dot(back, r_ref[head, tensor * SIDE : (tensor + 1) * SIDE, :])
            ref[:, columns_of(head)] = (n_ref[tensor, :, columns_of(head)].astype(F32) + part).astype(BF)


def call(kernel, name, out, specs, scratch=(), flops=0, moved=0, places=None, limit=16):
    return pl.pallas_call(
        kernel,
        name=name,
        out_shape=out,
        in_specs=specs,
        out_specs=jax.tree.map(lambda _: VMEM, out) if places is None else places,
        scratch_shapes=list(scratch),
        cost_estimate=pl.CostEstimate(flops=flops, bytes_accessed=moved, transcendentals=0),
        compiler_params=pltpu.CompilerParams(vmem_limit_bytes=limit * 1024 * 1024),
    )


def shape(dims, dtype=BF):
    return jax.ShapeDtypeStruct(dims, dtype)


RING_GROUPS = [[base + i for i in range(RING)] for base in range(0, DEVICES, RING)]
DEPTH_GROUPS = [
    [y * 128 + z * 8 + i for z in range(DEPTH)] for y in range(ROWS) for i in range(RING)
]
ROW_GROUPS = [[y * 128 + i for y in range(ROWS)] for i in range(128)]


def exchange(array, groups):
    return lax.all_to_all(array, "seq", 0, 0, axis_index_groups=groups, tiled=True)


def partner(array, bit):
    return lax.ppermute(array, "seq", [(i, i ^ bit) for i in range(DEVICES)])


def body(query_rows, key_rows, value_rows, attn_out, out_grad, log_norms):
    index = lax.axis_index("seq").astype(jnp.int32).reshape(1)
    whole = (TOK, HEADS * WIDTH)
    side, stats = call(
        select_kernel,
        "select_rows",
        (shape((HEADS, CHUNK, WIDTH)), shape((16, HEADS * WIDTH))),
        [SMEM] + [ANY] * 6,
        [pltpu.VMEM(whole, BF)] * 5
        + [pltpu.VMEM((HEADS, TOK), F32), pltpu.SemaphoreType.DMA((6, 2))],
        flops=2 * 128 * 128 * 4096,
        moved=3 << 20,
        limit=60,
    )(index, query_rows, key_rows, value_rows, out_grad, attn_out, log_norms)
    side = exchange(side, RING_GROUPS)
    core, chip = call(
        payload_kernel,
        "near_payload",
        (shape((NEAR, HEADS * WIDTH)), shape((NEAR, HEADS * WIDTH))),
        [SMEM] + [ANY] * 5,
        [pltpu.SemaphoreType.DMA((2, 3))],
        moved=4 << 20,
        places=(ANY, ANY),
    )(index, query_rows, key_rows, value_rows, out_grad, stats)
    core, chip, relay = partner(core, 1), partner(chip, 2), partner(chip, 3)
    far, mine, pair = call(
        middle_kernel,
        "middle_rows",
        (shape((DEPTH, FAR, WIDTH)), shape((FAR, WIDTH)), shape((PAIR, WIDTH))),
        [SMEM, VMEM],
        [pltpu.VMEM((144, 128), F32)],
        moved=1 << 20,
    )(index, side)
    far = exchange(far, DEPTH_GROUPS)
    pair = partner(pair, 8)
    sums = call(
        pair_kernel,
        "pair_grads",
        shape((RING, OUT_CHUNK, WIDTH), F32),
        [SMEM, VMEM, VMEM, ANY],
        flops=8 * 2 * 10 * 128 * 256 * 256,
        moved=1 << 20,
    )(index, side, pair, chip)
    plane = call(
        plane_kernel,
        "plane_rows",
        shape((ROWS, PLANE, WIDTH)),
        [SMEM, VMEM, ANY],
        moved=1 << 20,
    )(index, far, sums)
    near_grads = call(
        near_kernel,
        "near_grads",
        shape((3, TOK, HEADS * WIDTH)),
        [SMEM] + [VMEM] * 8 + [ANY],
        flops=int(1 * 2 * 128 * 128 * 128 * 8 * 17),
        moved=4 << 20,
    )(index, query_rows, key_rows, value_rows, out_grad, stats, core, chip, relay, plane)
    plane = exchange(plane, ROW_GROUPS)
    grads = call(
        join_kernel,
        "join_grads",
        shape((RING, OUT_CHUNK, WIDTH)),
        [SMEM, VMEM, VMEM, VMEM, ANY],
        [pltpu.VMEM((RING, OUT_CHUNK, WIDTH), F32), pltpu.VMEM((128, 128), F32)],
        moved=1 << 20,
    )(index, plane, mine, sums, near_grads)
    grads = exchange(grads, RING_GROUPS)
    out = shape(whole)
    return call(
        post_kernel,
        "add_levels",
        (out, out, out),
        [VMEM] * 2,
        flops=2 * 128 * 32 * 3072,
        moved=4 << 20,
    )(grads, near_grads)


def solution(mesh):
    return jax.shard_map(
        body,
        mesh=mesh,
        in_specs=(
            P("seq", None),
            P("seq", None),
            P("seq", None),
            P("seq", None),
            P("seq", None),
            P(None, "seq"),
        ),
        out_specs=(P("seq", None), P("seq", None), P("seq", None)),
        check_vma=False,
    )
```
